512 devices in a mesh: factor: 32 (over x, z_hi, core), rows: 16 (over z_lo, y).
Axes of the slice: x: 4, y: 4, z: 16 (z_hi: 4, z_lo: 4; z = z_hi * 4 + z_lo), core: 2. Of those that a mesh axis runs over, the one named last changes fastest.
Arguments:
- working: bfloat16 [16384, 16384], P('rows', 'factor'), may hold values from -30 to 30, as said below
- levels: int32 [3, 32, 512], P(None, 'factor'), may hold values from 0 to 511, each once within a row
Outputs:
- rotated: bfloat16 [16384, 16384], P('rows', 'factor')
The draws below stay inside these ranges and needn't reach their ends.
Inputs may be any that keep to these rules, and one draw needn't show every extreme that they name: `working`: entries of order one; column scales differ over the columns. Each row levels[s, p, :] is a permutation of 0 to 511.
All inputs are finite; a program needn't handle non-finite values.
Results may differ from the reference program's by a relative error of at most 0.013.
The reference program's roundings to bfloat16 on the way (of `paired` and `rotation`) count: a program that leaves them out, or rounds other values in their place, can miss the bound.
Values may be sent and summed in bfloat16 or wider, within the bound.
A program may use at most 64 MiB of HBM per device.

```python
import math
import jax
import jax.numpy as jnp
from jax import lax

BLK = 256
STEPS = 3
ORDER = 16384
N_FACTOR = 32


def draw_working(key, part):
    key = jax.random.fold_in(key, 11)
    first, second = jax.random.split(key, 2)
    columns = jnp.exp(jax.random.uniform(second, (1, ORDER), jnp.float32, 0.0, math.log(3.0)))
    base = jax.random.truncated_normal(first, -4.0, 4.0, (ORDER, ORDER), jnp.float32)
    return (base * columns).astype(jnp.bfloat16)


def setup_inputs(seed: int = 0) -> dict:
    key_of = jax.random.split(jax.random.key(seed), 3)
    return {
        "working": draw_working(jax.random.fold_in(key_of[2], 71), 0),
        "levels": jax.vmap(lambda own: jax.random.permutation(own, 2 * BLK))(jax.random.split(key_of[1], STEPS * N_FACTOR)).reshape((STEPS, N_FACTOR, 2 * BLK)).astype(jnp.int32),
    }


def rotate_pair(paired, levels_row):
    width = paired.shape[1]
    wide = paired.astype(jnp.float32)
    gram = jnp.dot(wide.T, wide, precision=lax.Precision.HIGHEST)
    spectrum = 1.0 + levels_row.astype(jnp.float32) / float(width)
    scaled = gram * spectrum[None, :]
    frobenius = jnp.sqrt(jnp.sum(scaled * scaled) + 1e-06)
    start = scaled * (0.5 * math.sqrt(width) / frobenius)
    inner = jnp.dot(start.T, start, precision=lax.Precision.HIGHEST)
    correct = 1.5 * jnp.eye(width, dtype=jnp.float32) - 0.5 * inner
    rotation = jnp.dot(start, correct, precision=lax.Precision.HIGHEST).astype(jnp.bfloat16)
    moved = jnp.dot(wide, rotation.astype(jnp.float32), precision=lax.Precision.HIGHEST)
    return moved.astype(jnp.bfloat16)

def reference(working, levels):
    width = 2 * BLK
    blocks = jnp.transpose(working.reshape(ORDER, N_FACTOR, width), (1, 0, 2))
    for sweep in range(STEPS):
        blocks = lax.map(lambda item: rotate_pair(item[0], item[1]), (blocks, levels[sweep]))
        if sweep + 1 < STEPS:
            upper = blocks[:, :, :BLK]
            lower = blocks[:, :, BLK:]
            new_upper = jnp.concatenate([upper[:1], lower[:1], upper[1:-1]], axis=0)
            new_lower = jnp.concatenate([lower[1:], upper[-1:]], axis=0)
            blocks = jnp.concatenate([new_upper, new_lower], axis=2)
    return jnp.transpose(blocks, (1, 0, 2)).reshape(ORDER, ORDER)
```

```python
import functools
import math

import jax
import jax.numpy as jnp
from jax import lax
from jax.experimental import pallas as pl
from jax.experimental.pallas import tpu as pltpu
from jax.sharding import PartitionSpec as P

MESH = pl.DeviceIdType.MESH
F32, BF16 = jnp.float32, jnp.bfloat16
Y_SIZE = 4
CHUNKS = 4


def inner_rows(left, right):
    return lax.dot_general(
        left, right, (((0,), (0,)), ((), ())), preferred_element_type=F32
    )


def mm(left, right):
    return jnp.dot(left, right, preferred_element_type=F32)


def halves(wide):
    high = wide.astype(BF16)
    return high, (wide - high.astype(F32)).astype(BF16)


def remote(src, dst, send, recv, **to):
    return pltpu.make_async_remote_copy(
        src_ref=src, dst_ref=dst, send_sem=send, recv_sem=recv, device_id=to, device_id_type=MESH
    )


def kernel(n_factor, n_rows, steps, working, levels, out,
           upper, lower, up_stage, down_stage, stage, part0, part, landed0, landed, gram0, cross,
           diag, diag_stage, gram, narrow, narrow_rest, square, square_rest, rotation,
           in_sem, out_sem, rs_send, rs_recv, ag_send, ag_recv, mv_send, mv_recv,
           dg_send, dg_recv, df_send, df_recv):
    f, r = lax.axis_index("factor"), lax.axis_index("rows")
    y = lax.rem(r, Y_SIZE)
    z_base = r - y
    height, half = upper.shape[1], upper.shape[2]
    width = 2 * half
    tall = height // CHUNKS
    above, below = lax.rem(f + 1, n_factor), lax.rem(f + n_factor - 1, n_factor)
    first, last = f == 0, f == n_factor - 1

    def peer(k):
        return lax.rem(r + k, n_rows)

    def peer_back(k):
        return lax.rem(r + n_rows - k, n_rows)

    load_u = pltpu.make_async_copy(working.at[:, pl.ds(0, half)], upper.at[0], in_sem.at[0])
    load_l = pltpu.make_async_copy(working.at[:, pl.ds(half, half)], lower.at[0], in_sem.at[1])
    load_u.start()
    load_l.start()
    barrier = pltpu.get_barrier_semaphore()
    for k in range(1, n_rows):
        pl.semaphore_signal(barrier, inc=1, device_id={"rows": peer(k)}, device_id_type=MESH)
    pl.semaphore_signal(barrier, inc=1, device_id={"factor": above}, device_id_type=MESH)
    pl.semaphore_signal(barrier, inc=1, device_id={"factor": below}, device_id_type=MESH)

    pending = []

    def reduce_rows(s, mine, landing, total):
        q = mine.shape[0] // n_rows

        def rows_of(device):
            return pl.ds(pl.multiple_of(device * q, q), q)

        def scatter(k):
            return remote(mine.at[rows_of(peer(k))], landing.at[k - 1],
                          rs_send.at[s, k], rs_recv.at[s, k], rows=peer(k))

        def gather(k, device):
            return remote(total.at[rows_of(device)], total.at[rows_of(device)],
                          ag_send.at[s, k], ag_recv.at[s, k], rows=peer(k))

        for k in range(1, n_rows):
            scatter(k).start()
        acc = mine[rows_of(r), :].astype(F32)
        for k in range(1, n_rows):
            scatter(k).wait_recv()
            acc = acc + landing[k - 1].astype(F32)
        total[rows_of(r), :] = acc.astype(total.dtype)
        for k in range(1, n_rows):
            gather(k, r).start()
        for k in range(1, n_rows):
            gather(k, peer_back(k)).wait_recv()
        pending.extend(functools.partial(scatter, k) for k in range(1, n_rows))
        pending.extend(functools.partial(gather, k, r) for k in range(1, n_rows))

    def solve(s):
        spectrum = 1.0 + levels[s].astype(F32) / float(width)
        squared = spectrum * spectrum
        norms = jnp.zeros((1, width), F32)
        for i in range(0, width, half):
            high = narrow[i:i + half, :]
            product = mm(high, narrow[...]) + mm(high, narrow_rest[...]) + mm(narrow_rest[i:i + half, :], narrow[...])
            square[i:i + half, :], square_rest[i:i + half, :] = halves(product)
            wide = gram[i:i + half, :]
            norms = norms + jnp.sum(wide * wide, axis=0, keepdims=True)
        total = jnp.sum(norms * squared, axis=1, keepdims=True)
        scale = (0.5 * math.sqrt(width)) / jnp.sqrt(total + 1e-06)
        outer = scale * spectrum
        cubic = (0.5 * scale * scale)
        for i in range(0, width, half):
            wide = gram[i:i + half, :]
            high, low = halves(wide * squared)
            third = mm(high, square[...]) + mm(high, square_rest[...]) + mm(low, square[...])
            rotation[i:i + half, :] = (outer * (1.5 * wide - cubic * third)).astype(BF16)

    def apply(s, c):
        rows = pl.ds(c * tall, tall)
        return mm(upper[s, rows, :], rotation[:half, :]) + mm(lower[s, rows, :], rotation[half:, :])

    def diag_slice(s, b, j):
        return diag.at[s, b, pl.ds(pl.multiple_of(j * (half // Y_SIZE), half // Y_SIZE), half // Y_SIZE)]

    def move_up(s, c):
        rows = pl.ds(c * tall, tall)
        return remote(up_stage.at[s, rows], upper.at[s + 1, rows], mv_send.at[s, 0, c], mv_recv.at[s, 0, c], factor=above)

    def move_down(s, c):
        rows = pl.ds(c * tall, tall)
        return remote(down_stage.at[s, rows], lower.at[s + 1, rows], mv_send.at[s, 1, c], mv_recv.at[s, 1, c], factor=below)

    def diag_up(s):
        own = pl.ds(pl.multiple_of(y * (half // Y_SIZE), half // Y_SIZE), half // Y_SIZE)
        return remote(diag_stage.at[s, 0, own], diag_slice(s, 0, y), dg_send.at[s, 0], dg_recv.at[s, 0], factor=above)

    def diag_down(s):
        own = pl.ds(pl.multiple_of(y * (half // Y_SIZE), half // Y_SIZE), half // Y_SIZE)
        return remote(diag_stage.at[s, 1, own], diag_slice(s, 1, y), dg_send.at[s, 1], dg_recv.at[s, 1], factor=below)

    def diag_spread(s, b, k, j):
        return remote(diag_slice(s, b, j), diag_slice(s, b, j), df_send.at[s, b, k], df_recv.at[s, b, k],
                      rows=z_base + lax.rem(y + k, Y_SIZE))

    def shift(s):
        for c in range(CHUNKS):
            rows = pl.ds(c * tall, tall)
            moved = apply(s, c)
            new_u, new_l = moved[:, :half], moved[:, half:]
            up_stage[s, rows, :] = jnp.where(first, new_l, new_u).astype(BF16)
            down_stage[s, rows, :] = new_l.astype(BF16)

            @pl.when(first)
            def _():
                upper[s + 1, rows, :] = new_u.astype(BF16)

            @pl.when(last)
            def _():
                lower[s + 1, rows, :] = new_u.astype(BF16)

            @pl.when(jnp.logical_not(last))
            def _():
                move_up(s, c).start()

            @pl.when(jnp.logical_not(first))
            def _():
                move_down(s, c).start()

            if c == 0:
                turned = mm(narrow[...], rotation[...]) + mm(narrow_rest[...], rotation[...])
                high, low = halves(turned)
                own_u = inner_rows(rotation[:, :half], high[:, :half]) + inner_rows(rotation[:, :half], low[:, :half])
                own_l = inner_rows(rotation[:, half:], high[:, half:]) + inner_rows(rotation[:, half:], low[:, half:])
                diag_stage[s, 0] = jnp.where(first, own_l, own_u)
                diag_stage[s, 1] = own_l
                diag_stage[s, 2] = own_u
                own = pl.ds(pl.multiple_of(y * (half // Y_SIZE), half // Y_SIZE), half // Y_SIZE)

                @pl.when(first)
                def _():
                    diag[s, 0, own, :] = diag_stage[s, 2, own, :]

                @pl.when(last)
                def _():
                    diag[s, 1, own, :] = diag_stage[s, 2, own, :]

                @pl.when(jnp.logical_not(last))
                def _():
                    diag_up(s).start()

                @pl.when(jnp.logical_not(first))
                def _():
                    diag_down(s).start()

        @pl.when(jnp.logical_not(first))
        def _():
            diag_up(s).wait_recv()

        for k in range(1, Y_SIZE):
            diag_spread(s, 0, k, y).start()

        @pl.when(jnp.logical_not(last))
        def _():
            diag_down(s).wait_recv()

        for k in range(1, Y_SIZE):
            diag_spread(s, 1, k, y).start()

        total = None
        for c in range(CHUNKS):
            rows = pl.ds(c * tall, tall)

            @pl.when(jnp.logical_not(first))
            def _():
                move_up(s, c).wait_recv()

            @pl.when(jnp.logical_not(last))
            def _():
                move_down(s, c).wait_recv()

            term = inner_rows(upper[s + 1, rows, :], lower[s + 1, rows, :])
            total = term if total is None else total + term
        part[s] = total.astype(BF16)

    load_u.wait()
    load_l.wait()
    part0[:half, :] = inner_rows(upper[0], upper[0]).astype(BF16)
    part0[half:width, :] = inner_rows(upper[0], lower[0]).astype(BF16)
    part0[width:, :] = inner_rows(lower[0], lower[0]).astype(BF16)
    pl.semaphore_wait(barrier, n_rows + 1)

    for s in range(steps):
        if s == 0:
            reduce_rows(s, part0, landed0, gram0)
            own_u, own_x, own_l = gram0[:half, :], gram0[half:width, :], gram0[width:, :]
        else:
            reduce_rows(s, part.at[s - 1], landed.at[s - 1], cross.at[s - 1])
            for b in range(2):
                for k in range(1, Y_SIZE):
                    diag_spread(s - 1, b, k, lax.rem(y + Y_SIZE - k, Y_SIZE)).wait_recv()
            own_u, own_x, own_l = diag[s - 1, 0], cross[s - 1], diag[s - 1, 1]
        gram[:half, :half] = own_u
        own_x = own_x.astype(F32)
        gram[:half, half:] = own_x
        gram[half:, :half] = own_x.T
        gram[half:, half:] = own_l
        narrow[...], narrow_rest[...] = halves(gram[...])
        solve(s)
        if s + 1 < steps:
            shift(s)

    stores = []
    for c in range(CHUNKS):
        rows = pl.ds(c * tall, tall)
        stage[rows, :] = apply(steps - 1, c).astype(BF16)
        store = pltpu.make_async_copy(stage.at[rows], out.at[rows], out_sem.at[c])
        store.start()
        stores.append(store)

    for copy in pending:
        copy().wait_send()
    for s in range(steps - 1):
        for c in range(CHUNKS):
            @pl.when(jnp.logical_not(last))
            def _():
                move_up(s, c).wait_send()

            @pl.when(jnp.logical_not(first))
            def _():
                move_down(s, c).wait_send()

        @pl.when(jnp.logical_not(last))
        def _():
            diag_up(s).wait_send()

        @pl.when(jnp.logical_not(first))
        def _():
            diag_down(s).wait_send()

        for b in range(2):
            for k in range(1, Y_SIZE):
                diag_spread(s, b, k, y).wait_send()
    for store in stores:
        store.wait()


def body(working, levels):
    height, width = working.shape
    half = width // 2
    steps = levels.shape[0]
    n_factor, n_rows = lax.axis_size("factor"), lax.axis_size("rows")
    dma = pltpu.SemaphoreType.DMA
    moves = steps - 1
    return pl.pallas_call(
        functools.partial(kernel, n_factor, n_rows, steps),
        out_shape=jax.ShapeDtypeStruct((height, width), BF16),
        in_specs=[pl.BlockSpec(memory_space=pl.ANY), pl.BlockSpec(memory_space=pltpu.VMEM)],
        out_specs=pl.BlockSpec(memory_space=pl.ANY),
        scratch_shapes=[
            pltpu.VMEM((steps, height, half), BF16),
            pltpu.VMEM((steps, height, half), BF16),
            pltpu.VMEM((moves, height, half), BF16),
            pltpu.VMEM((moves, height, half), BF16),
            pltpu.VMEM((height, width), BF16),
            pltpu.VMEM((3 * half, half), BF16),
            pltpu.VMEM((moves, half, half), BF16),
            pltpu.VMEM((n_rows - 1, 3 * half // n_rows, half), BF16),
            pltpu.VMEM((moves, n_rows - 1, half // n_rows, half), BF16),
            pltpu.VMEM((3 * half, half), F32),
            pltpu.VMEM((moves, half, half), BF16),
            pltpu.VMEM((moves, 2, half, half), F32),
            pltpu.VMEM((moves, 3, half, half), F32),
            pltpu.VMEM((width, width), F32),
            pltpu.VMEM((width, width), BF16),
            pltpu.VMEM((width, width), BF16),
            pltpu.VMEM((width, width), BF16),
            pltpu.VMEM((width, width), BF16),
            pltpu.VMEM((width, width), BF16),
            dma((2,)),
            dma((CHUNKS,)),
            dma((steps, n_rows)),
            dma((steps, n_rows)),
            dma((steps, n_rows)),
            dma((steps, n_rows)),
            dma((moves, 2, CHUNKS)),
            dma((moves, 2, CHUNKS)),
            dma((moves, 2)),
            dma((moves, 2)),
            dma((moves, 2, Y_SIZE)),
            dma((moves, 2, Y_SIZE)),
        ],
        compiler_params=pltpu.CompilerParams(
            collective_id=0, has_side_effects=True, vmem_limit_bytes=40 << 20
        ),
        cost_estimate=pl.CostEstimate(
            flops=steps * 4 * height * width * width, bytes_accessed=4 * height * width, transcendentals=0
        ),
        name="jacobi",
    )(working, levels)


def solution(mesh):
    placed = (P("rows", "factor"), P(None, "factor", None))
    return jax.shard_map(
        body, mesh=mesh, in_specs=placed, out_specs=P("rows", "factor"), check_vma=False
    )
```

```python
import functools
import math

import jax
import jax.numpy as jnp
from jax import lax
from jax.experimental import pallas as pl
from jax.experimental.pallas import tpu as pltpu
from jax.sharding import PartitionSpec as P

MESH = pl.DeviceIdType.MESH
F32, BF16 = jnp.float32, jnp.bfloat16
Y_SIZE = 4
CHUNKS = 4


def inner_rows(left, right):
    return lax.dot_general(
        left, right, (((0,), (0,)), ((), ())), preferred_element_type=F32
    )


def mm(left, right):
    return jnp.dot(left, right, preferred_element_type=F32)


def halves(wide):
    high = wide.astype(BF16)
    return high, (wide - high.astype(F32)).astype(BF16)


def remote(src, dst, send, recv, **to):
    return pltpu.make_async_remote_copy(
        src_ref=src, dst_ref=dst, send_sem=send, recv_sem=recv, device_id=to, device_id_type=MESH
    )


def kernel(n_factor, n_rows, steps, working, levels_in, out,
           levels, blocks, outs, part0, part, landed0, landed, gram0, cross,
           own_squares, squares, diag, diag_stage, gram, narrow, narrow_rest, square, square_rest, rotation,
           in_sem, sq_send, sq_recv, rs_send, rs_recv, ag_send, ag_recv, agz_send, agz_recv, agy_send, agy_recv, mv_send, mv_recv,
           dg_send, dg_recv, df_send, df_recv):
    f, r = lax.axis_index("factor"), lax.axis_index("rows")
    y = lax.rem(r, Y_SIZE)
    z = r // Y_SIZE
    z_size = n_rows // Y_SIZE
    height, half = blocks.shape[2], blocks.shape[3]
    width = 2 * half
    tall = height // CHUNKS
    above, below = lax.rem(f + 1, n_factor), lax.rem(f + n_factor - 1, n_factor)
    first, last = f == 0, f == n_factor - 1
    not_first, not_last = f > 0, f < n_factor - 1

    def peer(k):
        return lax.rem(r + k, n_rows)

    def peer_back(k):
        return lax.rem(r + n_rows - k, n_rows)

    loads = [pltpu.make_async_copy(working.at[:, pl.ds(b * half, half)], blocks.at[0, b], in_sem.at[b]) for b in range(2)]
    loads.append(pltpu.make_async_copy(levels_in, levels, in_sem.at[2]))
    for load in loads:
        load.start()
    barrier = pltpu.get_barrier_semaphore()
    for k in range(1, n_rows):
        pl.semaphore_signal(barrier, inc=1, device_id={"rows": peer(k)}, device_id_type=MESH)
    for to in (above, below):
        pl.semaphore_signal(barrier, inc=1, device_id={"factor": to}, device_id_type=MESH)

    sent = []

    def start(copy, when=None):
        if when is None:
            copy().start()
        else:
            @pl.when(when)
            def _():
                copy().start()
        sent.append((copy, when))

    def landed_on(copy, when=None):
        if when is None:
            copy().wait_recv()
        else:
            @pl.when(when)
            def _():
                copy().wait_recv()

    def scatter_rows(s, mine, landing, meanwhile=None):
        q = mine.shape[0] // n_rows

        def rows_of(device):
            return pl.ds(pl.multiple_of(device * q, q), q)

        def scatter(k):
            return remote(mine.at[rows_of(peer(k))], landing.at[k - 1],
                          rs_send.at[s, k], rs_recv.at[s, k], rows=peer(k))

        for k in range(1, n_rows):
            start(functools.partial(scatter, k))
        if meanwhile is not None:
            meanwhile()
        acc = mine[rows_of(r), :].astype(F32)
        for k in range(1, n_rows):
            scatter(k).wait_recv()
            acc = acc + landing[k - 1].astype(F32)
        return acc, rows_of

    def gather_rows(s, acc, rows_of, total):
        def gather(k, device):
            return remote(total.at[rows_of(device)], total.at[rows_of(device)],
                          ag_send.at[s, k], ag_recv.at[s, k], rows=peer(k))

        total[rows_of(r), :] = acc.astype(total.dtype)
        for k in range(1, n_rows):
            start(functools.partial(gather, k, r))
        for k in range(1, n_rows):
            gather(k, peer_back(k)).wait_recv()

    def gather_rows_by_axes(s, acc, rows_of, total):
        def along_z(k, device):
            return remote(total.at[rows_of(device)], total.at[rows_of(device)], agz_send.at[s, k], agz_recv.at[s, k],
                          rows=lax.rem(z + k, z_size) * Y_SIZE + y)

        def along_y(k, j, device):
            return remote(total.at[rows_of(device)], total.at[rows_of(device)], agy_send.at[s, k, j], agy_recv.at[s, k, j],
                          rows=z * Y_SIZE + lax.rem(y + j, Y_SIZE))

        def at(k, j):
            return lax.rem(z + z_size - k, z_size) * Y_SIZE + lax.rem(y + Y_SIZE - j, Y_SIZE)

        total[rows_of(r), :] = acc.astype(total.dtype)
        for k in range(1, z_size):
            start(functools.partial(along_z, k, r))
        for k in range(z_size):
            if k:
                along_z(k, at(k, 0)).wait_recv()
            for j in range(1, Y_SIZE):
                start(functools.partial(along_y, k, j, at(k, 0)))
        for k in range(z_size):
            for j in range(1, Y_SIZE):
                along_y(k, j, at(k, j)).wait_recv()

    def solve(s):
        spectrum = 1.0 + levels[s].astype(F32) / float(width)
        squared = spectrum * spectrum
        norms = jnp.zeros((1, width), F32)
        for i in range(0, width, half):
            high = narrow[i:i + half, :]
            product = mm(high, narrow[...]) + mm(high, narrow_rest[...]) + mm(narrow_rest[i:i + half, :], narrow[...])
            square[i:i + half, :], square_rest[i:i + half, :] = halves(product)
            wide = gram[i:i + half, :]
            norms = norms + jnp.sum(wide * wide, axis=0, keepdims=True)
        total = jnp.sum(norms * squared, axis=1, keepdims=True)
        scale = (0.5 * math.sqrt(width)) / jnp.sqrt(total + 1e-06)
        outer = scale * spectrum
        cubic = (0.5 * scale * scale)
        for i in range(0, width, half):
            wide = gram[i:i + half, :]
            high, low = halves(wide * squared)
            third = mm(high, square[...]) + mm(high, square_rest[...]) + mm(low, square[...])
            result = (outer * (1.5 * wide - cubic * third)).astype(BF16)
            rotation[s, 0, i:i + half, :] = result[:, :half]
            rotation[s, 1, i:i + half, :] = result[:, half:]

    def apply(s, rows, b):
        return mm(blocks[s, 0, rows, :], rotation[s, b, :half, :]) + mm(blocks[s, 1, rows, :], rotation[s, b, half:, :])

    quarter = half // Y_SIZE

    def quarter_of(j):
        return pl.ds(pl.multiple_of(j * quarter, quarter), quarter)

    def diag_move(s, b):
        return remote(diag_stage.at[s, b, quarter_of(y)], diag.at[s, b, quarter_of(y)],
                      dg_send.at[s, b], dg_recv.at[s, b], factor=above if b == 0 else below)

    def diag_spread(s, b, k, j):
        return remote(diag.at[s, b, quarter_of(j)], diag.at[s, b, quarter_of(j)], df_send.at[s, b, k], df_recv.at[s, b, k],
                      rows=z * Y_SIZE + lax.rem(y + k, Y_SIZE))

    def send_diag(s):
        turned = []
        for b in range(2):
            turned.append(halves(mm(narrow[...], rotation[s, b]) + mm(narrow_rest[...], rotation[s, b])))
        own_u, own_l = (inner_rows(rotation[s, b], turned[b][0]) + inner_rows(rotation[s, b], turned[b][1]) for b in range(2))
        diag_stage[s, 0] = jnp.where(first, own_l, own_u)
        diag_stage[s, 1] = own_l
        diag_stage[s, 2] = own_u

        @pl.when(first)
        def _():
            diag[s, 0, quarter_of(y), :] = diag_stage[s, 2, quarter_of(y), :]

        @pl.when(last)
        def _():
            diag[s, 1, quarter_of(y), :] = diag_stage[s, 2, quarter_of(y), :]

        start(functools.partial(diag_move, s, 0), not_last)
        start(functools.partial(diag_move, s, 1), not_first)

    def spread_diag(s):
        for b in range(2):
            landed_on(functools.partial(diag_move, s, b), not_first if b == 0 else not_last)
            for k in range(1, Y_SIZE):
                start(functools.partial(diag_spread, s, b, k, y))

    def chunk(c):
        return pl.ds(c * tall, tall)

    def move(s, c, b):
        return remote(outs.at[s, b, chunk(c)], blocks.at[s + 1, b, chunk(c)], mv_send.at[s, b, c], mv_recv.at[s, b, c],
                      factor=above if b == 0 else below)

    def rotate_and_send(s):
        for c in range(CHUNKS):
            new_u, new_l = apply(s, chunk(c), 0), apply(s, chunk(c), 1)
            outs[s, 0, chunk(c), :] = jnp.where(first, new_l, new_u).astype(BF16)
            outs[s, 1, chunk(c), :] = new_l.astype(BF16)

            @pl.when(first)
            def _():
                blocks[s + 1, 0, chunk(c), :] = new_u.astype(BF16)

            @pl.when(last)
            def _():
                blocks[s + 1, 1, chunk(c), :] = new_u.astype(BF16)

            start(functools.partial(move, s, c, 0), not_last)
            start(functools.partial(move, s, c, 1), not_first)
        send_diag(s)

    def cross_of(s):
        total = None
        for c in range(CHUNKS):
            landed_on(functools.partial(move, s - 1, c, 0), not_first)
            landed_on(functools.partial(move, s - 1, c, 1), not_last)
            term = inner_rows(blocks[s, 0, chunk(c), :], blocks[s, 1, chunk(c), :])
            total = term if total is None else total + term
        return total

    def back(k):
        return lax.rem(y + Y_SIZE - k, Y_SIZE)

    def finish_gram(s, own_x):
        for b in range(2):
            for k in range(1, Y_SIZE):
                diag_spread(s, b, k, back(k)).wait_recv()
        own_x = own_x.astype(F32)
        gram[:half, :half] = diag[s, 0]
        gram[:half, half:] = own_x
        gram[half:, :half] = own_x.T
        gram[half:, half:] = diag[s, 1]
        narrow[...], narrow_rest[...] = halves(gram[...])

    for load in loads:
        load.wait()
    tile = half // 2
    corners = [(0, 0), (0, 1), (1, 1)]
    every = [(0, 0), (0, 1), (1, 0), (1, 1)]
    spots = [(0, 0, c) for c in corners] + [(0, 1, c) for c in every] + [(1, 1, c) for c in corners]
    products = {(a, b): inner_rows(blocks[0, a], blocks[0, b]).astype(BF16) for a, b in ((0, 0), (0, 1), (1, 1))}
    for n, (a, b, (i, j)) in enumerate(spots):
        part0[n * tile:(n + 1) * tile, :] = products[a, b][i * tile:(i + 1) * tile, j * tile:(j + 1) * tile]
    pl.semaphore_wait(barrier, n_rows + 1)
    own_squares[...] = jnp.zeros_like(own_squares)
    for b in range(2):
        wide = blocks[0, b].astype(F32)
        sums = jnp.sum(wide * wide, axis=0, keepdims=True)
        for i in range(2):
            own_squares[2 * b + i:2 * b + i + 1, :] = sums[:, i * tile:(i + 1) * tile]

    def spread_squares(k):
        return remote(own_squares, squares.at[k - 1], sq_send.at[k], sq_recv.at[k], rows=peer(k))

    def send_squares():
        for k in range(1, n_rows):
            start(functools.partial(spread_squares, k))

    acc, rows_of = scatter_rows(0, part0, landed0, send_squares)
    gather_rows_by_axes(0, acc, rows_of, gram0)
    for n, (a, b, (i, j)) in enumerate(spots):
        row, col = a * half + i * tile, b * half + j * tile
        piece = gram0[n * tile:(n + 1) * tile, :]
        gram[row:row + tile, col:col + tile] = piece
        if row != col:
            gram[col:col + tile, row:row + tile] = piece.T
    sums = own_squares[...]
    for k in range(1, n_rows):
        spread_squares(k).wait_recv()
        sums = sums + squares[k - 1]
    on_diagonal = lax.broadcasted_iota(jnp.int32, (tile, tile), 0) == lax.broadcasted_iota(jnp.int32, (tile, tile), 1)
    for i in range(2 * half // tile):
        at = slice(i * tile, (i + 1) * tile)
        gram[at, at] = jnp.where(on_diagonal, sums[i:i + 1, :], gram[at, at])
    narrow[...], narrow_rest[...] = halves(gram[...])
    solve(0)
    rotate_and_send(0)

    part[0] = cross_of(1).astype(BF16)
    acc, rows_of = scatter_rows(1, part.at[0], landed.at[0], lambda: spread_diag(0))
    gather_rows(0, acc, rows_of, cross.at[0])
    finish_gram(0, cross[0])
    solve(1)
    rotate_and_send(1)

    part[1] = cross_of(2).astype(BF16)
    acc, rows_of = scatter_rows(2, part.at[1], landed.at[1], lambda: spread_diag(1))
    gather_rows(1, acc, rows_of, cross.at[1])
    finish_gram(1, cross[1])
    solve(2)
    for c in range(CHUNKS):
        for b in range(2):
            out[chunk(c), b * half:(b + 1) * half] = apply(2, chunk(c), b).astype(BF16)

    for copy, when in sent:
        if when is None:
            copy().wait_send()
        else:
            @pl.when(when)
            def _():
                copy().wait_send()


def body(working, levels):
    height, width = working.shape
    half = width // 2
    steps = levels.shape[0]
    n_factor, n_rows = lax.axis_size("factor"), lax.axis_size("rows")
    dma = pltpu.SemaphoreType.DMA
    moves = steps - 1
    triangle = 10 * half // 2
    pairs = lambda *shape: [dma(shape), dma(shape)]
    return pl.pallas_call(
        functools.partial(kernel, n_factor, n_rows, steps),
        out_shape=jax.ShapeDtypeStruct((height, width), BF16),
        in_specs=[pl.BlockSpec(memory_space=pltpu.HBM), pl.BlockSpec(memory_space=pltpu.HBM)],
        out_specs=pl.BlockSpec(memory_space=pltpu.VMEM),
        scratch_shapes=[
            pltpu.VMEM(levels.shape, jnp.int32),
            pltpu.VMEM((steps, 2, height, half), BF16),
            pltpu.VMEM((moves, 2, height, half), BF16),
            pltpu.VMEM((triangle, half // 2), BF16),
            pltpu.VMEM((moves, half, half), BF16),
            pltpu.VMEM((n_rows - 1, triangle // n_rows, half // 2), BF16),
            pltpu.VMEM((moves, n_rows - 1, half // n_rows, half), BF16),
            pltpu.VMEM((triangle, half // 2), F32),
            pltpu.VMEM((moves, half, half), BF16),
            pltpu.VMEM((8, half // 2), F32),
            pltpu.VMEM((n_rows - 1, 8, half // 2), F32),
            pltpu.VMEM((moves, 2, half, half), F32),
            pltpu.VMEM((moves, 3, half, half), F32),
            pltpu.VMEM((width, width), F32),
            pltpu.VMEM((width, width), BF16),
            pltpu.VMEM((width, width), BF16),
            pltpu.VMEM((width, width), BF16),
            pltpu.VMEM((width, width), BF16),
            pltpu.VMEM((steps, 2, width, half), BF16),
            dma((3,)),
            *pairs(n_rows),
            *pairs(steps, n_rows),
            *pairs(moves, n_rows),
            *pairs(steps, n_rows // Y_SIZE),
            *pairs(steps, n_rows // Y_SIZE, Y_SIZE),
            *pairs(moves, 2, CHUNKS),
            *pairs(moves, 2),
            *pairs(moves, 2, Y_SIZE),
        ],
        compiler_params=pltpu.CompilerParams(
            collective_id=0, has_side_effects=True, vmem_limit_bytes=48 << 20
        ),
        cost_estimate=pl.CostEstimate(
            flops=steps * 4 * height * width * width, bytes_accessed=4 * height * width, transcendentals=0
        ),
        name="jacobi",
    )(working, levels)


def solution(mesh):
    placed = (P("rows", "factor"), P(None, "factor", None))
    return jax.shard_map(
        body, mesh=mesh, in_specs=placed, out_specs=P("rows", "factor"), check_vma=False
    )
```

```python
import functools
import math

import jax
import jax.numpy as jnp
from jax import lax
from jax.experimental import pallas as pl
from jax.experimental.pallas import tpu as pltpu
from jax.sharding import PartitionSpec as P

MESH = pl.DeviceIdType.MESH
F32, BF16 = jnp.float32, jnp.bfloat16
Y_SIZE = 4
CHUNKS = 4


def inner_rows(left, right):
    return lax.dot_general(
        left, right, (((0,), (0,)), ((), ())), preferred_element_type=F32
    )


def mm(left, right):
    return jnp.dot(left, right, preferred_element_type=F32)


def halves(wide):
    high = wide.astype(BF16)
    return high, (wide - high.astype(F32)).astype(BF16)


def remote(src, dst, send, recv, **to):
    return pltpu.make_async_remote_copy(
        src_ref=src, dst_ref=dst, send_sem=send, recv_sem=recv, device_id=to, device_id_type=MESH
    )


def kernel(n_factor, n_rows, steps, working, levels_in, out,
           levels, blocks, outs, part0, part, landed0, landed, gram0, cross,
           own_squares, squares, diag, diag_stage, line, line_stage, gram, narrow, narrow_rest, square, square_rest, rotation,
           in_sem, sq_send, sq_recv, rs_send, rs_recv, ag_send, ag_recv, agz_send, agz_recv, agy_send, agy_recv, mv_send, mv_recv,
           dg_send, dg_recv, df_send, df_recv, ln_send, ln_recv):
    f, r = lax.axis_index("factor"), lax.axis_index("rows")
    y = lax.rem(r, Y_SIZE)
    z = r // Y_SIZE
    z_size = n_rows // Y_SIZE
    height, half = blocks.shape[2], blocks.shape[3]
    width = 2 * half
    tall = height // CHUNKS
    above, below = lax.rem(f + 1, n_factor), lax.rem(f + n_factor - 1, n_factor)
    first, last = f == 0, f == n_factor - 1
    not_first, not_last = f > 0, f < n_factor - 1

    def peer(k):
        return lax.rem(r + k, n_rows)

    def peer_back(k):
        return lax.rem(r + n_rows - k, n_rows)

    loads = [pltpu.make_async_copy(working.at[:, pl.ds(b * half, half)], blocks.at[0, b], in_sem.at[b]) for b in range(2)]
    loads.append(pltpu.make_async_copy(levels_in, levels, in_sem.at[2]))
    for load in loads:
        load.start()
    barrier = pltpu.get_barrier_semaphore()
    for k in range(1, n_rows):
        pl.semaphore_signal(barrier, inc=1, device_id={"rows": peer(k)}, device_id_type=MESH)
    for to in (above, below):
        pl.semaphore_signal(barrier, inc=1, device_id={"factor": to}, device_id_type=MESH)

    on_diagonal = lax.broadcasted_iota(jnp.int32, (half, half), 0) == lax.broadcasted_iota(jnp.int32, (half, half), 1)
    sent = []

    def start(copy, when=None):
        if when is None:
            copy().start()
        else:
            @pl.when(when)
            def _():
                copy().start()
        sent.append((copy, when))

    def landed_on(copy, when=None):
        if when is None:
            copy().wait_recv()
        else:
            @pl.when(when)
            def _():
                copy().wait_recv()

    def scatter_rows(s, mine, landing, meanwhile=None):
        q = mine.shape[0] // n_rows

        def rows_of(device):
            return pl.ds(pl.multiple_of(device * q, q), q)

        def scatter(k):
            return remote(mine.at[rows_of(peer(k))], landing.at[k - 1],
                          rs_send.at[s, k], rs_recv.at[s, k], rows=peer(k))

        for k in range(1, n_rows):
            start(functools.partial(scatter, k))
        if meanwhile is not None:
            meanwhile()
        acc = mine[rows_of(r), :].astype(F32)
        for k in range(1, n_rows):
            scatter(k).wait_recv()
            acc = acc + landing[k - 1].astype(F32)
        return acc, rows_of

    def gather_rows(s, acc, rows_of, total):
        def gather(k, device):
            return remote(total.at[rows_of(device)], total.at[rows_of(device)],
                          ag_send.at[s, k], ag_recv.at[s, k], rows=peer(k))

        total[rows_of(r), :] = acc.astype(total.dtype)
        for k in range(1, n_rows):
            start(functools.partial(gather, k, r))
        for k in range(1, n_rows):
            gather(k, peer_back(k)).wait_recv()

    def gather_rows_by_axes(s, acc, rows_of, total):
        def along_z(k, device):
            return remote(total.at[rows_of(device)], total.at[rows_of(device)], agz_send.at[s, k], agz_recv.at[s, k],
                          rows=lax.rem(z + k, z_size) * Y_SIZE + y)

        def along_y(k, j, device):
            return remote(total.at[rows_of(device)], total.at[rows_of(device)], agy_send.at[s, k, j], agy_recv.at[s, k, j],
                          rows=z * Y_SIZE + lax.rem(y + j, Y_SIZE))

        def at(k, j):
            return lax.rem(z + z_size - k, z_size) * Y_SIZE + lax.rem(y + Y_SIZE - j, Y_SIZE)

        total[rows_of(r), :] = acc.astype(total.dtype)
        for k in range(1, z_size):
            start(functools.partial(along_z, k, r))
        for k in range(z_size):
            if k:
                along_z(k, at(k, 0)).wait_recv()
            for j in range(1, Y_SIZE):
                start(functools.partial(along_y, k, j, at(k, 0)))
        for k in range(z_size):
            for j in range(1, Y_SIZE):
                along_y(k, j, at(k, j)).wait_recv()

    def solve(s):
        spectrum = 1.0 + levels[s].astype(F32) / float(width)
        squared = spectrum * spectrum
        norms = jnp.zeros((1, width), F32)
        for i in range(0, width, half):
            wide = gram[i:i + half, :] * spectrum
            norms = norms + jnp.sum(wide * wide, axis=0, keepdims=True)
        norm = jnp.sqrt(jnp.sum(norms, axis=1, keepdims=True) + 1e-06)
        scale = (0.5 * math.sqrt(width)) / norm
        for i in range(0, width, half):
            narrow[i:i + half, :], narrow_rest[i:i + half, :] = halves(gram[i:i + half, :] * scale)
        for i in range(0, width, half):
            high = narrow[i:i + half, :]
            product = mm(high, narrow[...]) + mm(high, narrow_rest[...]) + mm(narrow_rest[i:i + half, :], narrow[...])
            square[i:i + half, :], square_rest[i:i + half, :] = halves(product)
        for i in range(0, width, half):
            wide = gram[i:i + half, :] * scale
            high, low = halves(wide * squared)
            third = mm(high, square[...]) + mm(high, square_rest[...]) + mm(low, square[...])
            result = (spectrum * (1.5 * wide - 0.5 * third)).astype(BF16)
            rotation[s, 0, i:i + half, :] = result[:, :half]
            rotation[s, 1, i:i + half, :] = result[:, half:]
        return norm / (0.5 * math.sqrt(width))

    def apply(s, rows, b):
        return mm(blocks[s, 0, rows, :], rotation[s, b, :half, :]) + mm(blocks[s, 1, rows, :], rotation[s, b, half:, :])

    quarter = half // Y_SIZE

    def quarter_of(j):
        return pl.ds(pl.multiple_of(j * quarter, quarter), quarter)

    def diag_move(s, b):
        return remote(diag_stage.at[s, b, quarter_of(y)], diag.at[s, b, quarter_of(y)],
                      dg_send.at[s, b], dg_recv.at[s, b], factor=above if b == 0 else below)

    def line_move(s, b):
        return remote(line_stage.at[s, b], line.at[s, b], ln_send.at[s, b], ln_recv.at[s, b], factor=above if b == 0 else below)

    def diag_spread(s, b, k, j):
        return remote(diag.at[s, b, quarter_of(j)], diag.at[s, b, quarter_of(j)], df_send.at[s, b, k], df_recv.at[s, b, k],
                      rows=z * Y_SIZE + lax.rem(y + k, Y_SIZE))

    def send_diag(s, size):
        turned = []
        for b in range(2):
            turned.append(halves(mm(narrow[...], rotation[s, b]) + mm(narrow_rest[...], rotation[s, b])))
        own_u, own_l = (size * (inner_rows(rotation[s, b], turned[b][0]) + inner_rows(rotation[s, b], turned[b][1]))
                        for b in range(2))
        line_u, line_l = (jnp.sum(jnp.where(on_diagonal, own, 0.0), axis=0, keepdims=True) for own in (own_u, own_l))
        for i, (own, own_line) in enumerate(((jnp.where(first, own_l, own_u), jnp.where(first, line_l, line_u)),
                                             (own_l, line_l), (own_u, line_u))):
            diag_stage[s, i] = own.astype(BF16)
            line_stage[s, i] = jnp.broadcast_to(own_line, (8, half))

        @pl.when(first)
        def _():
            diag[s, 0, quarter_of(y), :] = diag_stage[s, 2, quarter_of(y), :]
            line[s, 0] = line_stage[s, 2]

        @pl.when(last)
        def _():
            diag[s, 1, quarter_of(y), :] = diag_stage[s, 2, quarter_of(y), :]
            line[s, 1] = line_stage[s, 2]

        start(functools.partial(diag_move, s, 0), not_last)
        start(functools.partial(diag_move, s, 1), not_first)
        start(functools.partial(line_move, s, 0), not_last)
        start(functools.partial(line_move, s, 1), not_first)

    def spread_diag(s):
        for b in range(2):
            landed_on(functools.partial(diag_move, s, b), not_first if b == 0 else not_last)
            for k in range(1, Y_SIZE):
                start(functools.partial(diag_spread, s, b, k, y))

    def chunk(c):
        return pl.ds(c * tall, tall)

    def move(s, c, b):
        return remote(outs.at[s, b, chunk(c)], blocks.at[s + 1, b, chunk(c)], mv_send.at[s, b, c], mv_recv.at[s, b, c],
                      factor=above if b == 0 else below)

    def rotate_and_send(s, size):
        for c in range(CHUNKS):
            new_u, new_l = apply(s, chunk(c), 0), apply(s, chunk(c), 1)
            outs[s, 0, chunk(c), :] = jnp.where(first, new_l, new_u).astype(BF16)
            outs[s, 1, chunk(c), :] = new_l.astype(BF16)

            @pl.when(first)
            def _():
                blocks[s + 1, 0, chunk(c), :] = new_u.astype(BF16)

            @pl.when(last)
            def _():
                blocks[s + 1, 1, chunk(c), :] = new_u.astype(BF16)

            start(functools.partial(move, s, c, 0), not_last)
            start(functools.partial(move, s, c, 1), not_first)
        send_diag(s, size)

    def cross_of(s):
        total = None
        for c in range(CHUNKS):
            landed_on(functools.partial(move, s - 1, c, 0), not_first)
            landed_on(functools.partial(move, s - 1, c, 1), not_last)
            term = inner_rows(blocks[s, 0, chunk(c), :], blocks[s, 1, chunk(c), :])
            total = term if total is None else total + term
        return total

    def back(k):
        return lax.rem(y + Y_SIZE - k, Y_SIZE)

    def finish_gram(s, own_x):
        for b in range(2):
            for k in range(1, Y_SIZE):
                diag_spread(s, b, k, back(k)).wait_recv()
            landed_on(functools.partial(line_move, s, b), not_first if b == 0 else not_last)
            at = slice(b * half, (b + 1) * half)
            gram[at, at] = jnp.where(on_diagonal, line[s, b, 0:1, :], diag[s, b].astype(F32))
        own_x = own_x.astype(F32)
        gram[:half, half:] = own_x
        gram[half:, :half] = own_x.T

    for load in loads:
        load.wait()
    tile = half // 2
    corners = [(0, 0), (0, 1), (1, 1)]
    every = [(0, 0), (0, 1), (1, 0), (1, 1)]
    spots = [(0, 0, c) for c in corners] + [(0, 1, c) for c in every] + [(1, 1, c) for c in corners]
    products = {(a, b): inner_rows(blocks[0, a], blocks[0, b]).astype(BF16) for a, b in ((0, 0), (0, 1), (1, 1))}
    for n, (a, b, (i, j)) in enumerate(spots):
        part0[n * tile:(n + 1) * tile, :] = products[a, b][i * tile:(i + 1) * tile, j * tile:(j + 1) * tile]
    pl.semaphore_wait(barrier, n_rows + 1)
    own_squares[...] = jnp.zeros_like(own_squares)
    for b in range(2):
        wide = blocks[0, b].astype(F32)
        sums = jnp.sum(wide * wide, axis=0, keepdims=True)
        for i in range(2):
            own_squares[2 * b + i:2 * b + i + 1, :] = sums[:, i * tile:(i + 1) * tile]

    def spread_squares(k):
        return remote(own_squares, squares.at[k - 1], sq_send.at[k], sq_recv.at[k], rows=peer(k))

    def send_squares():
        for k in range(1, n_rows):
            start(functools.partial(spread_squares, k))

    acc, rows_of = scatter_rows(0, part0, landed0, send_squares)
    gather_rows_by_axes(0, acc, rows_of, gram0)
    for n, (a, b, (i, j)) in enumerate(spots):
        row, col = a * half + i * tile, b * half + j * tile
        piece = gram0[n * tile:(n + 1) * tile, :].astype(F32)
        gram[row:row + tile, col:col + tile] = piece
        if row != col:
            gram[col:col + tile, row:row + tile] = piece.T
    sums = own_squares[...]
    for k in range(1, n_rows):
        spread_squares(k).wait_recv()
        sums = sums + squares[k - 1]
    for i in range(2 * half // tile):
        at = slice(i * tile, (i + 1) * tile)
        gram[at, at] = jnp.where(on_diagonal[:tile, :tile], sums[i:i + 1, :], gram[at, at])
    size = solve(0)
    rotate_and_send(0, size)

    part[0] = cross_of(1).astype(BF16)
    acc, rows_of = scatter_rows(1, part.at[0], landed.at[0], lambda: spread_diag(0))
    gather_rows(0, acc, rows_of, cross.at[0])
    finish_gram(0, cross[0])
    rotate_and_send(1, solve(1))

    part[1] = cross_of(2).astype(BF16)
    acc, rows_of = scatter_rows(2, part.at[1], landed.at[1], lambda: spread_diag(1))
    gather_rows(1, acc, rows_of, cross.at[1])
    finish_gram(1, cross[1])
    solve(2)
    for c in range(CHUNKS):
        for b in range(2):
            out[chunk(c), b * half:(b + 1) * half] = apply(2, chunk(c), b).astype(BF16)

    for copy, when in sent:
        if when is None:
            copy().wait_send()
        else:
            @pl.when(when)
            def _():
                copy().wait_send()


def body(working, levels):
    height, width = working.shape
    half = width // 2
    steps = levels.shape[0]
    n_factor, n_rows = lax.axis_size("factor"), lax.axis_size("rows")
    dma = pltpu.SemaphoreType.DMA
    moves = steps - 1
    triangle = 10 * half // 2
    pairs = lambda *shape: [dma(shape), dma(shape)]
    return pl.pallas_call(
        functools.partial(kernel, n_factor, n_rows, steps),
        out_shape=jax.ShapeDtypeStruct((height, width), BF16),
        in_specs=[pl.BlockSpec(memory_space=pltpu.HBM), pl.BlockSpec(memory_space=pltpu.HBM)],
        out_specs=pl.BlockSpec(memory_space=pltpu.VMEM),
        scratch_shapes=[
            pltpu.VMEM(levels.shape, jnp.int32),
            pltpu.VMEM((steps, 2, height, half), BF16),
            pltpu.VMEM((moves, 2, height, half), BF16),
            pltpu.VMEM((triangle, half // 2), BF16),
            pltpu.VMEM((moves, half, half), BF16),
            pltpu.VMEM((n_rows - 1, triangle // n_rows, half // 2), BF16),
            pltpu.VMEM((moves, n_rows - 1, half // n_rows, half), BF16),
            pltpu.VMEM((triangle, half // 2), BF16),
            pltpu.VMEM((moves, half, half), BF16),
            pltpu.VMEM((8, half // 2), F32),
            pltpu.VMEM((n_rows - 1, 8, half // 2), F32),
            pltpu.VMEM((moves, 2, half, half), BF16),
            pltpu.VMEM((moves, 3, half, half), BF16),
            pltpu.VMEM((moves, 2, 8, half), F32),
            pltpu.VMEM((moves, 3, 8, half), F32),
            pltpu.VMEM((width, width), F32),
            pltpu.VMEM((width, width), BF16),
            pltpu.VMEM((width, width), BF16),
            pltpu.VMEM((width, width), BF16),
            pltpu.VMEM((width, width), BF16),
            pltpu.VMEM((steps, 2, width, half), BF16),
            dma((3,)),
            *pairs(n_rows),
            *pairs(steps, n_rows),
            *pairs(moves, n_rows),
            *pairs(steps, n_rows // Y_SIZE),
            *pairs(steps, n_rows // Y_SIZE, Y_SIZE),
            *pairs(moves, 2, CHUNKS),
            *pairs(moves, 2),
            *pairs(moves, 2, Y_SIZE),
            *pairs(moves, 2),
        ],
        compiler_params=pltpu.CompilerParams(
            collective_id=0, has_side_effects=True, vmem_limit_bytes=52 << 20
        ),
        cost_estimate=pl.CostEstimate(
            flops=steps * 4 * height * width * width, bytes_accessed=4 * height * width, transcendentals=0
        ),
        name="jacobi",
    )(working, levels)


def solution(mesh):
    placed = (P("rows", "factor"), P(None, "factor", None))
    return jax.shard_map(
        body, mesh=mesh, in_specs=placed, out_specs=P("rows", "factor"), check_vma=False
    )
```

```python
import functools
import math

import jax
import jax.numpy as jnp
from jax import lax
from jax.experimental import pallas as pl
from jax.experimental.pallas import tpu as pltpu
from jax.sharding import PartitionSpec as P

MESH = pl.DeviceIdType.MESH
F32, BF16 = jnp.float32, jnp.bfloat16
Y_SIZE = 4
CHUNKS = 4


def inner_rows(left, right):
    return lax.dot_general(
        left, right, (((0,), (0,)), ((), ())), preferred_element_type=F32
    )


def mm(left, right):
    return jnp.dot(left, right, preferred_element_type=F32)


def halves(wide):
    high = wide.astype(BF16)
    return high, (wide - high.astype(F32)).astype(BF16)


def remote(src, dst, send, recv, **to):
    return pltpu.make_async_remote_copy(
        src_ref=src, dst_ref=dst, send_sem=send, recv_sem=recv, device_id=to, device_id_type=MESH
    )


def kernel(n_factor, n_rows, steps, working, levels_in, out,
           levels, blocks, outs, part0, part, landed0, landed, gram0, cross,
           own_squares, squares, diag, diag_stage, line, line_stage, gram, narrow, narrow_rest, square, square_rest, rotation,
           in_sem, sq_send, sq_recv, rs_send, rs_recv, agz_send, agz_recv, agy_send, agy_recv, mv_send, mv_recv,
           dg_send, dg_recv, df_send, df_recv, ln_send, ln_recv):
    f, r = lax.axis_index("factor"), lax.axis_index("rows")
    y = lax.rem(r, Y_SIZE)
    z = r // Y_SIZE
    z_size = n_rows // Y_SIZE
    height, half = blocks.shape[2], blocks.shape[3]
    width = 2 * half
    tall = height // CHUNKS
    above, below = lax.rem(f + 1, n_factor), lax.rem(f + n_factor - 1, n_factor)
    first, last = f == 0, f == n_factor - 1
    not_first, not_last = f > 0, f < n_factor - 1

    def peer(k):
        return lax.rem(r + k, n_rows)

    def peer_back(k):
        return lax.rem(r + n_rows - k, n_rows)

    loads = [pltpu.make_async_copy(working.at[:, pl.ds(b * half, half)], blocks.at[0, b], in_sem.at[b]) for b in range(2)]
    loads.append(pltpu.make_async_copy(levels_in, levels, in_sem.at[2]))
    for load in loads:
        load.start()
    barrier = pltpu.get_barrier_semaphore()
    for k in range(1, n_rows):
        pl.semaphore_signal(barrier, inc=1, device_id={"rows": peer(k)}, device_id_type=MESH)
    for to in (above, below):
        pl.semaphore_signal(barrier, inc=1, device_id={"factor": to}, device_id_type=MESH)

    on_diagonal = lax.broadcasted_iota(jnp.int32, (half, half), 0) == lax.broadcasted_iota(jnp.int32, (half, half), 1)
    sent = []

    def start(copy, when=None):
        if when is None:
            copy().start()
        else:
            @pl.when(when)
            def _():
                copy().start()
        sent.append((copy, when))

    def landed_on(copy, when=None):
        if when is None:
            copy().wait_recv()
        else:
            @pl.when(when)
            def _():
                copy().wait_recv()

    def scatter_rows(s, mine, landing, meanwhile=None):
        q = mine.shape[0] // n_rows

        def rows_of(device):
            return pl.ds(pl.multiple_of(device * q, q), q)

        def scatter(k):
            return remote(mine.at[rows_of(peer(k))], landing.at[k - 1],
                          rs_send.at[s, k], rs_recv.at[s, k], rows=peer(k))

        for k in range(1, n_rows):
            start(functools.partial(scatter, k))
        if meanwhile is not None:
            meanwhile()
        acc = mine[rows_of(r), :].astype(F32)
        for k in range(1, n_rows):
            scatter(k).wait_recv()
            acc = acc + landing[k - 1].astype(F32)
        return acc, rows_of

    def gather_rows(s, acc, rows_of, total, meanwhile):
        def along_z(k, device):
            return remote(total.at[rows_of(device)], total.at[rows_of(device)], agz_send.at[s, k], agz_recv.at[s, k],
                          rows=lax.rem(z + k, z_size) * Y_SIZE + y)

        def along_y(k, j, device):
            return remote(total.at[rows_of(device)], total.at[rows_of(device)], agy_send.at[s, k, j], agy_recv.at[s, k, j],
                          rows=z * Y_SIZE + lax.rem(y + j, Y_SIZE))

        def at(k, j):
            return lax.rem(z + z_size - k, z_size) * Y_SIZE + lax.rem(y + Y_SIZE - j, Y_SIZE)

        total[rows_of(r), :] = acc.astype(total.dtype)
        for k in range(1, z_size):
            start(functools.partial(along_z, k, r))
        for k in range(z_size):
            if k:
                along_z(k, at(k, 0)).wait_recv()
            for j in range(1, Y_SIZE):
                start(functools.partial(along_y, k, j, at(k, 0)))
        meanwhile()
        for k in range(z_size):
            for j in range(1, Y_SIZE):
                along_y(k, j, at(k, j)).wait_recv()

    def solve(s):
        spectrum = 1.0 + levels[s].astype(F32) / float(width)
        squared = spectrum * spectrum
        norms = jnp.zeros((1, width), F32)
        for i in range(0, width, half):
            wide = gram[i:i + half, :] * spectrum
            norms = norms + jnp.sum(wide * wide, axis=0, keepdims=True)
        norm = jnp.sqrt(jnp.sum(norms, axis=1, keepdims=True) + 1e-06)
        scale = (0.5 * math.sqrt(width)) / norm
        for i in range(0, width, half):
            narrow[i:i + half, :], narrow_rest[i:i + half, :] = halves(gram[i:i + half, :] * scale)
        for i in range(0, width, half):
            high = narrow[i:i + half, :]
            product = mm(high, narrow[...]) + mm(high, narrow_rest[...]) + mm(narrow_rest[i:i + half, :], narrow[...])
            square[i:i + half, :], square_rest[i:i + half, :] = halves(product)
        for i in range(0, width, half):
            wide = gram[i:i + half, :] * scale
            high, low = halves(wide * squared)
            third = mm(high, square[...]) + mm(high, square_rest[...]) + mm(low, square[...])
            result = (spectrum * (1.5 * wide - 0.5 * third)).astype(BF16)
            rotation[s, 0, i:i + half, :] = result[:, :half]
            rotation[s, 1, i:i + half, :] = result[:, half:]
        return norm / (0.5 * math.sqrt(width))

    def apply(s, rows, b):
        return mm(blocks[s, 0, rows, :], rotation[s, b, :half, :]) + mm(blocks[s, 1, rows, :], rotation[s, b, half:, :])

    quarter = half // Y_SIZE

    def quarter_of(j):
        return pl.ds(pl.multiple_of(j * quarter, quarter), quarter)

    def diag_move(s, b):
        return remote(diag_stage.at[s, b, quarter_of(y)], diag.at[s, b, quarter_of(y)],
                      dg_send.at[s, b], dg_recv.at[s, b], factor=above if b == 0 else below)

    def line_move(s, b):
        return remote(line_stage.at[s, b], line.at[s, b], ln_send.at[s, b], ln_recv.at[s, b], factor=above if b == 0 else below)

    def diag_spread(s, b, k, j):
        return remote(diag.at[s, b, quarter_of(j)], diag.at[s, b, quarter_of(j)], df_send.at[s, b, k], df_recv.at[s, b, k],
                      rows=z * Y_SIZE + lax.rem(y + k, Y_SIZE))

    def make_diag(s, size):
        turned = []
        for b in range(2):
            turned.append(halves(mm(narrow[...], rotation[s, b]) + mm(narrow_rest[...], rotation[s, b])))
        own_u, own_l = (size * (inner_rows(rotation[s, b], turned[b][0]) + inner_rows(rotation[s, b], turned[b][1]))
                        for b in range(2))
        line_u, line_l = (jnp.sum(jnp.where(on_diagonal, own, 0.0), axis=0, keepdims=True) for own in (own_u, own_l))
        for i, (own, own_line) in enumerate(((jnp.where(first, own_l, own_u), jnp.where(first, line_l, line_u)),
                                             (own_l, line_l), (own_u, line_u))):
            diag_stage[s, i] = own.astype(BF16)
            line_stage[s, i] = jnp.broadcast_to(own_line, (8, half))

        @pl.when(first)
        def _():
            diag[s, 0, quarter_of(y), :] = diag_stage[s, 2, quarter_of(y), :]
            line[s, 0] = line_stage[s, 2]

        @pl.when(last)
        def _():
            diag[s, 1, quarter_of(y), :] = diag_stage[s, 2, quarter_of(y), :]
            line[s, 1] = line_stage[s, 2]

    def send_diag(s):
        for moved in (diag_move, line_move):
            start(functools.partial(moved, s, 0), not_last)
            start(functools.partial(moved, s, 1), not_first)

    def spread_diag(s):
        for b in range(2):
            landed_on(functools.partial(diag_move, s, b), not_first if b == 0 else not_last)
            for k in range(1, Y_SIZE):
                start(functools.partial(diag_spread, s, b, k, y))

    def chunk(c):
        return pl.ds(c * tall, tall)

    def move(s, c, b):
        return remote(outs.at[s, b, chunk(c)], blocks.at[s + 1, b, chunk(c)], mv_send.at[s, b, c], mv_recv.at[s, b, c],
                      factor=above if b == 0 else below)

    def rotate_and_send(s, size):
        for c in range(CHUNKS):
            new_u, new_l = apply(s, chunk(c), 0), apply(s, chunk(c), 1)
            outs[s, 0, chunk(c), :] = jnp.where(first, new_l, new_u).astype(BF16)
            outs[s, 1, chunk(c), :] = new_l.astype(BF16)

            @pl.when(first)
            def _():
                blocks[s + 1, 0, chunk(c), :] = new_u.astype(BF16)

            @pl.when(last)
            def _():
                blocks[s + 1, 1, chunk(c), :] = new_u.astype(BF16)

            start(functools.partial(move, s, c, 0), not_last)
            start(functools.partial(move, s, c, 1), not_first)
        make_diag(s, size)

    def cross_of(s):
        total = None
        for c in range(CHUNKS):
            landed_on(functools.partial(move, s - 1, c, 0), not_first)
            landed_on(functools.partial(move, s - 1, c, 1), not_last)
            term = inner_rows(blocks[s, 0, chunk(c), :], blocks[s, 1, chunk(c), :])
            total = term if total is None else total + term
        return total

    def back(k):
        return lax.rem(y + Y_SIZE - k, Y_SIZE)

    def finish_gram(s, own_x):
        for b in range(2):
            for k in range(1, Y_SIZE):
                diag_spread(s, b, k, back(k)).wait_recv()
            landed_on(functools.partial(line_move, s, b), not_first if b == 0 else not_last)
            at = slice(b * half, (b + 1) * half)
            gram[at, at] = jnp.where(on_diagonal, line[s, b, 0:1, :], diag[s, b].astype(F32))
        own_x = own_x.astype(F32)
        gram[:half, half:] = own_x
        gram[half:, :half] = own_x.T

    for load in loads:
        load.wait()
    tile = half // 2
    corners = [(0, 0), (0, 1), (1, 1)]
    every = [(0, 0), (0, 1), (1, 0), (1, 1)]
    spots = [(0, 0, c) for c in corners] + [(0, 1, c) for c in every] + [(1, 1, c) for c in corners]
    products = {(a, b): inner_rows(blocks[0, a], blocks[0, b]).astype(BF16) for a, b in ((0, 0), (0, 1), (1, 1))}
    for n, (a, b, (i, j)) in enumerate(spots):
        part0[n * tile:(n + 1) * tile, :] = products[a, b][i * tile:(i + 1) * tile, j * tile:(j + 1) * tile]
    pl.semaphore_wait(barrier, n_rows + 1)
    def spread_squares(k):
        return remote(own_squares, squares.at[k - 1], sq_send.at[k], sq_recv.at[k], rows=peer(k))

    def send_squares():
        own_squares[...] = jnp.zeros_like(own_squares)
        for b in range(2):
            wide = blocks[0, b].astype(F32)
            sums = jnp.sum(wide * wide, axis=0, keepdims=True)
            for i in range(2):
                own_squares[2 * b + i:2 * b + i + 1, :] = sums[:, i * tile:(i + 1) * tile]
        for k in range(1, n_rows):
            start(functools.partial(spread_squares, k))

    acc, rows_of = scatter_rows(0, part0, landed0)
    gather_rows(0, acc, rows_of, gram0, send_squares)
    for n, (a, b, (i, j)) in enumerate(spots):
        row, col = a * half + i * tile, b * half + j * tile
        piece = gram0[n * tile:(n + 1) * tile, :].astype(F32)
        gram[row:row + tile, col:col + tile] = piece
        if row != col:
            gram[col:col + tile, row:row + tile] = piece.T
    sums = own_squares[...]
    for k in range(1, n_rows):
        spread_squares(k).wait_recv()
        sums = sums + squares[k - 1]
    for i in range(2 * half // tile):
        at = slice(i * tile, (i + 1) * tile)
        gram[at, at] = jnp.where(on_diagonal[:tile, :tile], sums[i:i + 1, :], gram[at, at])
    size = solve(0)
    rotate_and_send(0, size)

    part[0] = cross_of(1).astype(BF16)
    acc, rows_of = scatter_rows(1, part.at[0], landed.at[0], lambda: send_diag(0))
    gather_rows(1, acc, rows_of, cross.at[0], lambda: spread_diag(0))
    finish_gram(0, cross[0])
    rotate_and_send(1, solve(1))

    part[1] = cross_of(2).astype(BF16)
    acc, rows_of = scatter_rows(2, part.at[1], landed.at[1], lambda: send_diag(1))
    gather_rows(2, acc, rows_of, cross.at[1], lambda: spread_diag(1))
    finish_gram(1, cross[1])
    solve(2)
    for c in range(CHUNKS):
        for b in range(2):
            out[chunk(c), b * half:(b + 1) * half] = apply(2, chunk(c), b).astype(BF16)

    for copy, when in sent:
        if when is None:
            copy().wait_send()
        else:
            @pl.when(when)
            def _():
                copy().wait_send()


def body(working, levels):
    height, width = working.shape
    half = width // 2
    steps = levels.shape[0]
    n_factor, n_rows = lax.axis_size("factor"), lax.axis_size("rows")
    dma = pltpu.SemaphoreType.DMA
    moves = steps - 1
    triangle = 10 * half // 2
    pairs = lambda *shape: [dma(shape), dma(shape)]
    return pl.pallas_call(
        functools.partial(kernel, n_factor, n_rows, steps),
        out_shape=jax.ShapeDtypeStruct((height, width), BF16),
        in_specs=[pl.BlockSpec(memory_space=pltpu.HBM), pl.BlockSpec(memory_space=pltpu.HBM)],
        out_specs=pl.BlockSpec(memory_space=pltpu.VMEM),
        scratch_shapes=[
            pltpu.VMEM(levels.shape, jnp.int32),
            pltpu.VMEM((steps, 2, height, half), BF16),
            pltpu.VMEM((moves, 2, height, half), BF16),
            pltpu.VMEM((triangle, half // 2), BF16),
            pltpu.VMEM((moves, half, half), BF16),
            pltpu.VMEM((n_rows - 1, triangle // n_rows, half // 2), BF16),
            pltpu.VMEM((moves, n_rows - 1, half // n_rows, half), BF16),
            pltpu.VMEM((triangle, half // 2), BF16),
            pltpu.VMEM((moves, half, half), BF16),
            pltpu.VMEM((8, half // 2), F32),
            pltpu.VMEM((n_rows - 1, 8, half // 2), F32),
            pltpu.VMEM((moves, 2, half, half), BF16),
            pltpu.VMEM((moves, 3, half, half), BF16),
            pltpu.VMEM((moves, 2, 8, half), F32),
            pltpu.VMEM((moves, 3, 8, half), F32),
            pltpu.VMEM((width, width), F32),
            pltpu.VMEM((width, width), BF16),
            pltpu.VMEM((width, width), BF16),
            pltpu.VMEM((width, width), BF16),
            pltpu.VMEM((width, width), BF16),
            pltpu.VMEM((steps, 2, width, half), BF16),
            dma((3,)),
            *pairs(n_rows),
            *pairs(steps, n_rows),
            *pairs(steps, n_rows // Y_SIZE),
            *pairs(steps, n_rows // Y_SIZE, Y_SIZE),
            *pairs(moves, 2, CHUNKS),
            *pairs(moves, 2),
            *pairs(moves, 2, Y_SIZE),
            *pairs(moves, 2),
        ],
        compiler_params=pltpu.CompilerParams(
            collective_id=0, has_side_effects=True, vmem_limit_bytes=52 << 20
        ),
        cost_estimate=pl.CostEstimate(
            flops=steps * 4 * height * width * width, bytes_accessed=4 * height * width, transcendentals=0
        ),
        name="jacobi",
    )(working, levels)


def solution(mesh):
    placed = (P("rows", "factor"), P(None, "factor", None))
    return jax.shard_map(
        body, mesh=mesh, in_specs=placed, out_specs=P("rows", "factor"), check_vma=False
    )
```

```python
import functools
import math

import jax
import jax.numpy as jnp
from jax import lax
from jax.experimental import pallas as pl
from jax.experimental.pallas import tpu as pltpu
from jax.sharding import PartitionSpec as P

MESH = pl.DeviceIdType.MESH
F32, BF16 = jnp.float32, jnp.bfloat16
Y_SIZE = 4
CHUNKS = 4


def inner_rows(left, right):
    return lax.dot_general(
        left, right, (((0,), (0,)), ((), ())), preferred_element_type=F32
    )


def mm(left, right):
    return jnp.dot(left, right, preferred_element_type=F32)


def halves(wide):
    high = wide.astype(BF16)
    return high, (wide - high.astype(F32)).astype(BF16)


def remote(src, dst, send, recv, **to):
    return pltpu.make_async_remote_copy(
        src_ref=src, dst_ref=dst, send_sem=send, recv_sem=recv, device_id=to, device_id_type=MESH
    )


def kernel(n_factor, n_rows, steps, working, levels_in, out,
           levels, blocks, outs, part0, part, landed0, landed, gram0, cross,
           own_squares, squares, diag, diag_stage, line, line_stage, gram, narrow, narrow_rest, square, square_rest, rotation,
           in_sem, sq_send, sq_recv, rs_send, rs_recv, ag_send, ag_recv, agz_send, agz_recv, agy_send, agy_recv, mv_send, mv_recv,
           dg_send, dg_recv, df_send, df_recv, ln_send, ln_recv):
    f, r = lax.axis_index("factor"), lax.axis_index("rows")
    y = lax.rem(r, Y_SIZE)
    z = r // Y_SIZE
    z_size = n_rows // Y_SIZE
    height, half = blocks.shape[2], blocks.shape[3]
    width = 2 * half
    tall = height // CHUNKS
    above, below = lax.rem(f + 1, n_factor), lax.rem(f + n_factor - 1, n_factor)
    first, last = f == 0, f == n_factor - 1
    not_first, not_last = f > 0, f < n_factor - 1

    def peer(k):
        return lax.rem(r + k, n_rows)

    def peer_back(k):
        return lax.rem(r + n_rows - k, n_rows)

    loads = [pltpu.make_async_copy(working.at[:, pl.ds(b * half, half)], blocks.at[0, b], in_sem.at[b]) for b in range(2)]
    loads.append(pltpu.make_async_copy(levels_in, levels, in_sem.at[2]))
    for load in loads:
        load.start()
    barrier = pltpu.get_barrier_semaphore()
    for k in range(1, n_rows):
        pl.semaphore_signal(barrier, inc=1, device_id={"rows": peer(k)}, device_id_type=MESH)
    for to in (above, below):
        pl.semaphore_signal(barrier, inc=1, device_id={"factor": to}, device_id_type=MESH)

    on_diagonal = lax.broadcasted_iota(jnp.int32, (half, half), 0) == lax.broadcasted_iota(jnp.int32, (half, half), 1)
    sent = []

    def start(copy, when=None):
        if when is None:
            copy().start()
        else:
            @pl.when(when)
            def _():
                copy().start()
        sent.append((copy, when))

    def landed_on(copy, when=None):
        if when is None:
            copy().wait_recv()
        else:
            @pl.when(when)
            def _():
                copy().wait_recv()

    def scatter_rows(s, mine, landing, meanwhile=None):
        q = mine.shape[0] // n_rows

        def rows_of(device):
            return pl.ds(pl.multiple_of(device * q, q), q)

        def scatter(k):
            return remote(mine.at[rows_of(peer(k))], landing.at[k - 1],
                          rs_send.at[s, k], rs_recv.at[s, k], rows=peer(k))

        for k in range(1, n_rows):
            start(functools.partial(scatter, k))
        if meanwhile is not None:
            meanwhile()
        acc = mine[rows_of(r), :].astype(F32)
        for k in range(1, n_rows):
            scatter(k).wait_recv()
            acc = acc + landing[k - 1].astype(F32)
        return acc, rows_of

    def gather_rows(s, acc, rows_of, total, meanwhile):
        def gather(k, device):
            return remote(total.at[rows_of(device)], total.at[rows_of(device)],
                          ag_send.at[s, k], ag_recv.at[s, k], rows=peer(k))

        total[rows_of(r), :] = acc.astype(total.dtype)
        for k in range(1, n_rows):
            start(functools.partial(gather, k, r))
        meanwhile()
        for k in range(1, n_rows):
            gather(k, peer_back(k)).wait_recv()

    def gather_rows_by_axes(s, acc, rows_of, total, meanwhile):
        def along_z(k, device):
            return remote(total.at[rows_of(device)], total.at[rows_of(device)], agz_send.at[s, k], agz_recv.at[s, k],
                          rows=lax.rem(z + k, z_size) * Y_SIZE + y)

        def along_y(k, j, device):
            return remote(total.at[rows_of(device)], total.at[rows_of(device)], agy_send.at[s, k, j], agy_recv.at[s, k, j],
                          rows=z * Y_SIZE + lax.rem(y + j, Y_SIZE))

        def at(k, j):
            return lax.rem(z + z_size - k, z_size) * Y_SIZE + lax.rem(y + Y_SIZE - j, Y_SIZE)

        total[rows_of(r), :] = acc.astype(total.dtype)
        for k in range(1, z_size):
            start(functools.partial(along_z, k, r))
        for k in range(z_size):
            if k:
                along_z(k, at(k, 0)).wait_recv()
            for j in range(1, Y_SIZE):
                start(functools.partial(along_y, k, j, at(k, 0)))
        meanwhile()
        for k in range(z_size):
            for j in range(1, Y_SIZE):
                along_y(k, j, at(k, j)).wait_recv()

    def solve(s):
        spectrum = 1.0 + levels[s].astype(F32) / float(width)
        squared = spectrum * spectrum
        norms = jnp.zeros((1, width), F32)
        for i in range(0, width, half):
            wide = gram[i:i + half, :] * spectrum
            norms = norms + jnp.sum(wide * wide, axis=0, keepdims=True)
        norm = jnp.sqrt(jnp.sum(norms, axis=1, keepdims=True) + 1e-06)
        scale = (0.5 * math.sqrt(width)) / norm
        for i in range(0, width, half):
            narrow[i:i + half, :], narrow_rest[i:i + half, :] = halves(gram[i:i + half, :] * scale)
        for i in range(0, width, half):
            high = narrow[i:i + half, :]
            product = mm(high, narrow[...]) + mm(high, narrow_rest[...]) + mm(narrow_rest[i:i + half, :], narrow[...])
            square[i:i + half, :], square_rest[i:i + half, :] = halves(product)
        for i in range(0, width, half):
            wide = gram[i:i + half, :] * scale
            high, low = halves(wide * squared)
            third = mm(high, square[...]) + mm(high, square_rest[...]) + mm(low, square[...])
            result = (spectrum * (1.5 * wide - 0.5 * third)).astype(BF16)
            rotation[s, 0, i:i + half, :] = result[:, :half]
            rotation[s, 1, i:i + half, :] = result[:, half:]
        return norm / (0.5 * math.sqrt(width))

    def apply(s, rows, b):
        return mm(blocks[s, 0, rows, :], rotation[s, b, :half, :]) + mm(blocks[s, 1, rows, :], rotation[s, b, half:, :])

    quarter = half // Y_SIZE

    def quarter_of(j):
        return pl.ds(pl.multiple_of(j * quarter, quarter), quarter)

    def diag_move(s, b):
        return remote(diag_stage.at[s, b, quarter_of(y)], diag.at[s, b, quarter_of(y)],
                      dg_send.at[s, b], dg_recv.at[s, b], factor=above if b == 0 else below)

    def line_move(s, b):
        return remote(line_stage.at[s, b], line.at[s, b], ln_send.at[s, b], ln_recv.at[s, b], factor=above if b == 0 else below)

    def diag_spread(s, b, k, j):
        return remote(diag.at[s, b, quarter_of(j)], diag.at[s, b, quarter_of(j)], df_send.at[s, b, k], df_recv.at[s, b, k],
                      rows=z * Y_SIZE + lax.rem(y + k, Y_SIZE))

    def make_diag(s, size):
        turned = []
        for b in range(2):
            turned.append(halves(mm(narrow[...], rotation[s, b]) + mm(narrow_rest[...], rotation[s, b])))
        own_u, own_l = (size * (inner_rows(rotation[s, b], turned[b][0]) + inner_rows(rotation[s, b], turned[b][1]))
                        for b in range(2))
        line_u, line_l = (jnp.sum(jnp.where(on_diagonal, own, 0.0), axis=0, keepdims=True) for own in (own_u, own_l))
        for i, (own, own_line) in enumerate(((jnp.where(first, own_l, own_u), jnp.where(first, line_l, line_u)),
                                             (own_l, line_l), (own_u, line_u))):
            diag_stage[s, i] = own.astype(BF16)
            line_stage[s, i] = jnp.broadcast_to(own_line, (8, half))

        @pl.when(first)
        def _():
            diag[s, 0, quarter_of(y), :] = diag_stage[s, 2, quarter_of(y), :]
            line[s, 0] = line_stage[s, 2]

        @pl.when(last)
        def _():
            diag[s, 1, quarter_of(y), :] = diag_stage[s, 2, quarter_of(y), :]
            line[s, 1] = line_stage[s, 2]

    def send_diag(s):
        for moved in (diag_move, line_move):
            start(functools.partial(moved, s, 0), not_last)
            start(functools.partial(moved, s, 1), not_first)

    def spread_diag(s):
        for b in range(2):
            landed_on(functools.partial(diag_move, s, b), not_first if b == 0 else not_last)
            for k in range(1, Y_SIZE):
                start(functools.partial(diag_spread, s, b, k, y))

    def chunk(c):
        return pl.ds(c * tall, tall)

    def move(s, c, b):
        return remote(outs.at[s, b, chunk(c)], blocks.at[s + 1, b, chunk(c)], mv_send.at[s, b, c], mv_recv.at[s, b, c],
                      factor=above if b == 0 else below)

    def rotate_and_send(s, size):
        for c in range(CHUNKS):
            new_u, new_l = apply(s, chunk(c), 0), apply(s, chunk(c), 1)
            outs[s, 0, chunk(c), :] = jnp.where(first, new_l, new_u).astype(BF16)
            outs[s, 1, chunk(c), :] = new_l.astype(BF16)

            @pl.when(first)
            def _():
                blocks[s + 1, 0, chunk(c), :] = new_u.astype(BF16)

            @pl.when(last)
            def _():
                blocks[s + 1, 1, chunk(c), :] = new_u.astype(BF16)

            start(functools.partial(move, s, c, 0), not_last)
            start(functools.partial(move, s, c, 1), not_first)
        make_diag(s, size)

    def cross_of(s):
        total = None
        for c in range(CHUNKS):
            landed_on(functools.partial(move, s - 1, c, 0), not_first)
            landed_on(functools.partial(move, s - 1, c, 1), not_last)
            term = inner_rows(blocks[s, 0, chunk(c), :], blocks[s, 1, chunk(c), :])
            total = term if total is None else total + term
        return total

    def back(k):
        return lax.rem(y + Y_SIZE - k, Y_SIZE)

    def finish_gram(s, own_x):
        for b in range(2):
            for k in range(1, Y_SIZE):
                diag_spread(s, b, k, back(k)).wait_recv()
            landed_on(functools.partial(line_move, s, b), not_first if b == 0 else not_last)
            at = slice(b * half, (b + 1) * half)
            gram[at, at] = jnp.where(on_diagonal, line[s, b, 0:1, :], diag[s, b].astype(F32))
        own_x = own_x.astype(F32)
        gram[:half, half:] = own_x
        gram[half:, :half] = own_x.T

    for load in loads:
        load.wait()
    tile = half // 2
    corners = [(0, 0), (0, 1), (1, 1)]
    every = [(0, 0), (0, 1), (1, 0), (1, 1)]
    spots = [(0, 0, c) for c in corners] + [(0, 1, c) for c in every] + [(1, 1, c) for c in corners]
    products = {(a, b): inner_rows(blocks[0, a], blocks[0, b]).astype(BF16) for a, b in ((0, 0), (0, 1), (1, 1))}
    for n, (a, b, (i, j)) in enumerate(spots):
        part0[n * tile:(n + 1) * tile, :] = products[a, b][i * tile:(i + 1) * tile, j * tile:(j + 1) * tile]
    pl.semaphore_wait(barrier, n_rows + 1)
    def spread_squares(k):
        return remote(own_squares, squares.at[k - 1], sq_send.at[k], sq_recv.at[k], rows=peer(k))

    def send_squares():
        own_squares[...] = jnp.zeros_like(own_squares)
        for b in range(2):
            wide = blocks[0, b].astype(F32)
            sums = jnp.sum(wide * wide, axis=0, keepdims=True)
            for i in range(2):
                own_squares[2 * b + i:2 * b + i + 1, :] = sums[:, i * tile:(i + 1) * tile]
        for k in range(1, n_rows):
            start(functools.partial(spread_squares, k))

    acc, rows_of = scatter_rows(0, part0, landed0)
    gather_rows_by_axes(0, acc, rows_of, gram0, send_squares)
    for n, (a, b, (i, j)) in enumerate(spots):
        row, col = a * half + i * tile, b * half + j * tile
        piece = gram0[n * tile:(n + 1) * tile, :].astype(F32)
        gram[row:row + tile, col:col + tile] = piece
        if row != col:
            gram[col:col + tile, row:row + tile] = piece.T
    sums = own_squares[...]
    for k in range(1, n_rows):
        spread_squares(k).wait_recv()
        sums = sums + squares[k - 1]
    for i in range(2 * half // tile):
        at = slice(i * tile, (i + 1) * tile)
        gram[at, at] = jnp.where(on_diagonal[:tile, :tile], sums[i:i + 1, :], gram[at, at])
    size = solve(0)
    rotate_and_send(0, size)

    part[0] = cross_of(1).astype(BF16)
    acc, rows_of = scatter_rows(1, part.at[0], landed.at[0], lambda: send_diag(0))
    gather_rows(0, acc, rows_of, cross.at[0], lambda: spread_diag(0))
    finish_gram(0, cross[0])
    rotate_and_send(1, solve(1))

    part[1] = cross_of(2).astype(BF16)
    acc, rows_of = scatter_rows(2, part.at[1], landed.at[1], lambda: send_diag(1))
    gather_rows(1, acc, rows_of, cross.at[1], lambda: spread_diag(1))
    finish_gram(1, cross[1])
    solve(2)
    for c in range(CHUNKS):
        for b in range(2):
            out[chunk(c), b * half:(b + 1) * half] = apply(2, chunk(c), b).astype(BF16)

    for copy, when in sent:
        if when is None:
            copy().wait_send()
        else:
            @pl.when(when)
            def _():
                copy().wait_send()


def body(working, levels):
    height, width = working.shape
    half = width // 2
    steps = levels.shape[0]
    n_factor, n_rows = lax.axis_size("factor"), lax.axis_size("rows")
    dma = pltpu.SemaphoreType.DMA
    moves = steps - 1
    triangle = 10 * half // 2
    pairs = lambda *shape: [dma(shape), dma(shape)]
    return pl.pallas_call(
        functools.partial(kernel, n_factor, n_rows, steps),
        out_shape=jax.ShapeDtypeStruct((height, width), BF16),
        in_specs=[pl.BlockSpec(memory_space=pltpu.HBM), pl.BlockSpec(memory_space=pltpu.HBM)],
        out_specs=pl.BlockSpec(memory_space=pltpu.VMEM),
        scratch_shapes=[
            pltpu.VMEM(levels.shape, jnp.int32),
            pltpu.VMEM((steps, 2, height, half), BF16),
            pltpu.VMEM((moves, 2, height, half), BF16),
            pltpu.VMEM((triangle, half // 2), BF16),
            pltpu.VMEM((moves, half, half), BF16),
            pltpu.VMEM((n_rows - 1, triangle // n_rows, half // 2), BF16),
            pltpu.VMEM((moves, n_rows - 1, half // n_rows, half), BF16),
            pltpu.VMEM((triangle, half // 2), BF16),
            pltpu.VMEM((moves, half, half), BF16),
            pltpu.VMEM((8, half // 2), F32),
            pltpu.VMEM((n_rows - 1, 8, half // 2), F32),
            pltpu.VMEM((moves, 2, half, half), BF16),
            pltpu.VMEM((moves, 3, half, half), BF16),
            pltpu.VMEM((moves, 2, 8, half), F32),
            pltpu.VMEM((moves, 3, 8, half), F32),
            pltpu.VMEM((width, width), F32),
            pltpu.VMEM((width, width), BF16),
            pltpu.VMEM((width, width), BF16),
            pltpu.VMEM((width, width), BF16),
            pltpu.VMEM((width, width), BF16),
            pltpu.VMEM((steps, 2, width, half), BF16),
            dma((3,)),
            *pairs(n_rows),
            *pairs(steps, n_rows),
            *pairs(moves, n_rows),
            *pairs(steps, n_rows // Y_SIZE),
            *pairs(steps, n_rows // Y_SIZE, Y_SIZE),
            *pairs(moves, 2, CHUNKS),
            *pairs(moves, 2),
            *pairs(moves, 2, Y_SIZE),
            *pairs(moves, 2),
        ],
        compiler_params=pltpu.CompilerParams(
            collective_id=0, has_side_effects=True, vmem_limit_bytes=52 << 20
        ),
        cost_estimate=pl.CostEstimate(
            flops=steps * 4 * height * width * width, bytes_accessed=4 * height * width, transcendentals=0
        ),
        name="jacobi",
    )(working, levels)


def solution(mesh):
    placed = (P("rows", "factor"), P(None, "factor", None))
    return jax.shard_map(
        body, mesh=mesh, in_specs=placed, out_specs=P("rows", "factor"), check_vma=False
    )
```

```python
import functools
import math

import jax
import jax.numpy as jnp
from jax import lax
from jax.experimental import pallas as pl
from jax.experimental.pallas import tpu as pltpu
from jax.sharding import PartitionSpec as P

MESH = pl.DeviceIdType.MESH
F32, BF16 = jnp.float32, jnp.bfloat16
Y_SIZE = 4
CHUNKS = 8


def inner_rows(left, right):
    return lax.dot_general(
        left, right, (((0,), (0,)), ((), ())), preferred_element_type=F32
    )


def mm(left, right):
    return jnp.dot(left, right, preferred_element_type=F32)


def halves(wide):
    high = wide.astype(BF16)
    return high, (wide - high.astype(F32)).astype(BF16)


def remote(src, dst, send, recv, **to):
    return pltpu.make_async_remote_copy(
        src_ref=src, dst_ref=dst, send_sem=send, recv_sem=recv, device_id=to, device_id_type=MESH
    )


def kernel(n_factor, n_rows, steps, working, levels_in, out,
           levels, blocks, outs, part0, part, landed0, landed, gram0, cross,
           own_squares, squares, diag, diag_stage, line, line_stage, gram, narrow, narrow_rest, square, square_rest, rotation,
           in_sem, sq_send, sq_recv, rs_send, rs_recv, ag_send, ag_recv, agz_send, agz_recv, agy_send, agy_recv, mv_send, mv_recv,
           dg_send, dg_recv, df_send, df_recv, ln_send, ln_recv):
    f, r = lax.axis_index("factor"), lax.axis_index("rows")
    y = lax.rem(r, Y_SIZE)
    z = r // Y_SIZE
    z_size = n_rows // Y_SIZE
    height, half = blocks.shape[2], blocks.shape[3]
    width = 2 * half
    tall = height // CHUNKS
    above, below = lax.rem(f + 1, n_factor), lax.rem(f + n_factor - 1, n_factor)
    first, last = f == 0, f == n_factor - 1
    not_first, not_last = f > 0, f < n_factor - 1

    def peer(k):
        return lax.rem(r + k, n_rows)

    def peer_back(k):
        return lax.rem(r + n_rows - k, n_rows)

    loads = [pltpu.make_async_copy(working.at[:, pl.ds(b * half, half)], blocks.at[0, b], in_sem.at[b]) for b in range(2)]
    loads.append(pltpu.make_async_copy(levels_in, levels, in_sem.at[2]))
    for load in loads:
        load.start()
    barrier = pltpu.get_barrier_semaphore()
    for k in range(1, n_rows):
        pl.semaphore_signal(barrier, inc=1, device_id={"rows": peer(k)}, device_id_type=MESH)
    for to in (above, below):
        pl.semaphore_signal(barrier, inc=1, device_id={"factor": to}, device_id_type=MESH)

    on_diagonal = lax.broadcasted_iota(jnp.int32, (half, half), 0) == lax.broadcasted_iota(jnp.int32, (half, half), 1)
    sent = []

    def start(copy, when=None):
        if when is None:
            copy().start()
        else:
            @pl.when(when)
            def _():
                copy().start()
        sent.append((copy, when))

    def landed_on(copy, when=None):
        if when is None:
            copy().wait_recv()
        else:
            @pl.when(when)
            def _():
                copy().wait_recv()

    def scatter_rows(s, mine, landing, meanwhile=None):
        q = mine.shape[0] // n_rows

        def rows_of(device):
            return pl.ds(pl.multiple_of(device * q, q), q)

        def scatter(k):
            return remote(mine.at[rows_of(peer(k))], landing.at[k - 1],
                          rs_send.at[s, k], rs_recv.at[s, k], rows=peer(k))

        for k in range(1, n_rows):
            start(functools.partial(scatter, k))
        if meanwhile is not None:
            meanwhile()
        acc = mine[rows_of(r), :].astype(F32)
        for k in range(1, n_rows):
            scatter(k).wait_recv()
            acc = acc + landing[k - 1].astype(F32)
        return acc, rows_of

    def gather_rows(s, acc, rows_of, total, meanwhile):
        def gather(k, device):
            return remote(total.at[rows_of(device)], total.at[rows_of(device)],
                          ag_send.at[s, k], ag_recv.at[s, k], rows=peer(k))

        total[rows_of(r), :] = acc.astype(total.dtype)
        for k in range(1, n_rows):
            start(functools.partial(gather, k, r))
        meanwhile()
        for k in range(1, n_rows):
            gather(k, peer_back(k)).wait_recv()

    def gather_rows_by_axes(s, acc, rows_of, total, meanwhile):
        def along_z(k, device):
            return remote(total.at[rows_of(device)], total.at[rows_of(device)], agz_send.at[s, k], agz_recv.at[s, k],
                          rows=lax.rem(z + k, z_size) * Y_SIZE + y)

        def along_y(k, j, device):
            return remote(total.at[rows_of(device)], total.at[rows_of(device)], agy_send.at[s, k, j], agy_recv.at[s, k, j],
                          rows=z * Y_SIZE + lax.rem(y + j, Y_SIZE))

        def at(k, j):
            return lax.rem(z + z_size - k, z_size) * Y_SIZE + lax.rem(y + Y_SIZE - j, Y_SIZE)

        total[rows_of(r), :] = acc.astype(total.dtype)
        for k in range(1, z_size):
            start(functools.partial(along_z, k, r))
        for k in range(z_size):
            if k:
                along_z(k, at(k, 0)).wait_recv()
            for j in range(1, Y_SIZE):
                start(functools.partial(along_y, k, j, at(k, 0)))
        meanwhile()
        for k in range(z_size):
            for j in range(1, Y_SIZE):
                along_y(k, j, at(k, j)).wait_recv()

    def solve(s):
        spectrum = 1.0 + levels[s].astype(F32) / float(width)
        squared = spectrum * spectrum
        norms = jnp.zeros((1, width), F32)
        for i in range(0, width, half):
            wide = gram[i:i + half, :] * spectrum
            norms = norms + jnp.sum(wide * wide, axis=0, keepdims=True)
        norm = jnp.sqrt(jnp.sum(norms, axis=1, keepdims=True) + 1e-06)
        scale = (0.5 * math.sqrt(width)) / norm
        for i in range(0, width, half):
            narrow[i:i + half, :], narrow_rest[i:i + half, :] = halves(gram[i:i + half, :] * scale)
        for i in range(0, width, half):
            high = narrow[i:i + half, :]
            product = mm(high, narrow[...]) + mm(high, narrow_rest[...]) + mm(narrow_rest[i:i + half, :], narrow[...])
            square[i:i + half, :], square_rest[i:i + half, :] = halves(product)
        for i in range(0, width, half):
            wide = gram[i:i + half, :] * scale
            high, low = halves(wide * squared)
            third = mm(high, square[...]) + mm(high, square_rest[...]) + mm(low, square[...])
            result = (spectrum * (1.5 * wide - 0.5 * third)).astype(BF16)
            rotation[s, 0, i:i + half, :] = result[:, :half]
            rotation[s, 1, i:i + half, :] = result[:, half:]
        return norm / (0.5 * math.sqrt(width))

    def apply(s, rows, b):
        return mm(blocks[s, 0, rows, :], rotation[s, b, :half, :]) + mm(blocks[s, 1, rows, :], rotation[s, b, half:, :])

    quarter = half // Y_SIZE

    def quarter_of(j):
        return pl.ds(pl.multiple_of(j * quarter, quarter), quarter)

    def diag_move(s, b):
        return remote(diag_stage.at[s, b, quarter_of(y)], diag.at[s, b, quarter_of(y)],
                      dg_send.at[s, b], dg_recv.at[s, b], factor=above if b == 0 else below)

    def line_move(s, b):
        return remote(line_stage.at[s, b], line.at[s, b], ln_send.at[s, b], ln_recv.at[s, b], factor=above if b == 0 else below)

    def diag_spread(s, b, k, j):
        return remote(diag.at[s, b, quarter_of(j)], diag.at[s, b, quarter_of(j)], df_send.at[s, b, k], df_recv.at[s, b, k],
                      rows=z * Y_SIZE + lax.rem(y + k, Y_SIZE))

    def make_diag(s, size):
        turned = []
        for b in range(2):
            turned.append(halves(mm(narrow[...], rotation[s, b]) + mm(narrow_rest[...], rotation[s, b])))
        own_u, own_l = (size * (inner_rows(rotation[s, b], turned[b][0]) + inner_rows(rotation[s, b], turned[b][1]))
                        for b in range(2))
        line_u, line_l = (jnp.sum(jnp.where(on_diagonal, own, 0.0), axis=0, keepdims=True) for own in (own_u, own_l))
        for i, (own, own_line) in enumerate(((jnp.where(first, own_l, own_u), jnp.where(first, line_l, line_u)),
                                             (own_l, line_l), (own_u, line_u))):
            diag_stage[s, i] = own.astype(BF16)
            line_stage[s, i] = jnp.broadcast_to(own_line, (8, half))

        @pl.when(first)
        def _():
            diag[s, 0, quarter_of(y), :] = diag_stage[s, 2, quarter_of(y), :]
            line[s, 0] = line_stage[s, 2]

        @pl.when(last)
        def _():
            diag[s, 1, quarter_of(y), :] = diag_stage[s, 2, quarter_of(y), :]
            line[s, 1] = line_stage[s, 2]

    def send_diag(s):
        for moved in (diag_move, line_move):
            start(functools.partial(moved, s, 0), not_last)
            start(functools.partial(moved, s, 1), not_first)

    def spread_diag(s):
        for b in range(2):
            landed_on(functools.partial(diag_move, s, b), not_first if b == 0 else not_last)
            for k in range(1, Y_SIZE):
                start(functools.partial(diag_spread, s, b, k, y))

    def chunk(c):
        return pl.ds(c * tall, tall)

    def move(s, c, b):
        return remote(outs.at[s, b, chunk(c)], blocks.at[s + 1, b, chunk(c)], mv_send.at[s, b, c], mv_recv.at[s, b, c],
                      factor=above if b == 0 else below)

    def rotate_and_send(s, size):
        for c in range(CHUNKS):
            new_u, new_l = apply(s, chunk(c), 0), apply(s, chunk(c), 1)
            outs[s, 0, chunk(c), :] = jnp.where(first, new_l, new_u).astype(BF16)
            outs[s, 1, chunk(c), :] = new_l.astype(BF16)

            @pl.when(first)
            def _():
                blocks[s + 1, 0, chunk(c), :] = new_u.astype(BF16)

            @pl.when(last)
            def _():
                blocks[s + 1, 1, chunk(c), :] = new_u.astype(BF16)

            start(functools.partial(move, s, c, 0), not_last)
            start(functools.partial(move, s, c, 1), not_first)
        make_diag(s, size)

    def cross_of(s):
        total = None
        for c in range(CHUNKS):
            landed_on(functools.partial(move, s - 1, c, 0), not_first)
            landed_on(functools.partial(move, s - 1, c, 1), not_last)
            term = inner_rows(blocks[s, 0, chunk(c), :], blocks[s, 1, chunk(c), :])
            total = term if total is None else total + term
        return total

    def back(k):
        return lax.rem(y + Y_SIZE - k, Y_SIZE)

    def finish_gram(s, own_x):
        for b in range(2):
            for k in range(1, Y_SIZE):
                diag_spread(s, b, k, back(k)).wait_recv()
            landed_on(functools.partial(line_move, s, b), not_first if b == 0 else not_last)
            at = slice(b * half, (b + 1) * half)
            gram[at, at] = jnp.where(on_diagonal, line[s, b, 0:1, :], diag[s, b].astype(F32))
        own_x = own_x.astype(F32)
        gram[:half, half:] = own_x
        gram[half:, :half] = own_x.T

    for load in loads:
        load.wait()
    tile = half // 2
    corners = [(0, 0), (0, 1), (1, 1)]
    every = [(0, 0), (0, 1), (1, 0), (1, 1)]
    spots = [(0, 0, c) for c in corners] + [(0, 1, c) for c in every] + [(1, 1, c) for c in corners]
    products = {(a, b): inner_rows(blocks[0, a], blocks[0, b]).astype(BF16) for a, b in ((0, 0), (0, 1), (1, 1))}
    for n, (a, b, (i, j)) in enumerate(spots):
        part0[n * tile:(n + 1) * tile, :] = products[a, b][i * tile:(i + 1) * tile, j * tile:(j + 1) * tile]
    pl.semaphore_wait(barrier, n_rows + 1)
    def spread_squares(k):
        return remote(own_squares, squares.at[k - 1], sq_send.at[k], sq_recv.at[k], rows=peer(k))

    def send_squares():
        own_squares[...] = jnp.zeros_like(own_squares)
        for b in range(2):
            wide = blocks[0, b].astype(F32)
            sums = jnp.sum(wide * wide, axis=0, keepdims=True)
            for i in range(2):
                own_squares[2 * b + i:2 * b + i + 1, :] = sums[:, i * tile:(i + 1) * tile]
        for k in range(1, n_rows):
            start(functools.partial(spread_squares, k))

    acc, rows_of = scatter_rows(0, part0, landed0)
    gather_rows_by_axes(0, acc, rows_of, gram0, send_squares)
    for n, (a, b, (i, j)) in enumerate(spots):
        row, col = a * half + i * tile, b * half + j * tile
        piece = gram0[n * tile:(n + 1) * tile, :].astype(F32)
        gram[row:row + tile, col:col + tile] = piece
        if row != col:
            gram[col:col + tile, row:row + tile] = piece.T
    sums = own_squares[...]
    for k in range(1, n_rows):
        spread_squares(k).wait_recv()
        sums = sums + squares[k - 1]
    for i in range(2 * half // tile):
        at = slice(i * tile, (i + 1) * tile)
        gram[at, at] = jnp.where(on_diagonal[:tile, :tile], sums[i:i + 1, :], gram[at, at])
    size = solve(0)
    rotate_and_send(0, size)

    part[0] = cross_of(1).astype(BF16)
    acc, rows_of = scatter_rows(1, part.at[0], landed.at[0], lambda: send_diag(0))
    gather_rows(0, acc, rows_of, cross.at[0], lambda: spread_diag(0))
    finish_gram(0, cross[0])
    rotate_and_send(1, solve(1))

    part[1] = cross_of(2).astype(BF16)
    acc, rows_of = scatter_rows(2, part.at[1], landed.at[1], lambda: send_diag(1))
    gather_rows(1, acc, rows_of, cross.at[1], lambda: spread_diag(1))
    finish_gram(1, cross[1])
    solve(2)
    for c in range(CHUNKS):
        for b in range(2):
            out[chunk(c), b * half:(b + 1) * half] = apply(2, chunk(c), b).astype(BF16)

    for copy, when in sent:
        if when is None:
            copy().wait_send()
        else:
            @pl.when(when)
            def _():
                copy().wait_send()


def body(working, levels):
    height, width = working.shape
    half = width // 2
    steps = levels.shape[0]
    n_factor, n_rows = lax.axis_size("factor"), lax.axis_size("rows")
    dma = pltpu.SemaphoreType.DMA
    moves = steps - 1
    triangle = 10 * half // 2
    pairs = lambda *shape: [dma(shape), dma(shape)]
    return pl.pallas_call(
        functools.partial(kernel, n_factor, n_rows, steps),
        out_shape=jax.ShapeDtypeStruct((height, width), BF16),
        in_specs=[pl.BlockSpec(memory_space=pltpu.HBM), pl.BlockSpec(memory_space=pltpu.HBM)],
        out_specs=pl.BlockSpec(memory_space=pltpu.VMEM),
        scratch_shapes=[
            pltpu.VMEM(levels.shape, jnp.int32),
            pltpu.VMEM((steps, 2, height, half), BF16),
            pltpu.VMEM((moves, 2, height, half), BF16),
            pltpu.VMEM((triangle, half // 2), BF16),
            pltpu.VMEM((moves, half, half), BF16),
            pltpu.VMEM((n_rows - 1, triangle // n_rows, half // 2), BF16),
            pltpu.VMEM((moves, n_rows - 1, half // n_rows, half), BF16),
            pltpu.VMEM((triangle, half // 2), BF16),
            pltpu.VMEM((moves, half, half), BF16),
            pltpu.VMEM((8, half // 2), F32),
            pltpu.VMEM((n_rows - 1, 8, half // 2), F32),
            pltpu.VMEM((moves, 2, half, half), BF16),
            pltpu.VMEM((moves, 3, half, half), BF16),
            pltpu.VMEM((moves, 2, 8, half), F32),
            pltpu.VMEM((moves, 3, 8, half), F32),
            pltpu.VMEM((width, width), F32),
            pltpu.VMEM((width, width), BF16),
            pltpu.VMEM((width, width), BF16),
            pltpu.VMEM((width, width), BF16),
            pltpu.VMEM((width, width), BF16),
            pltpu.VMEM((steps, 2, width, half), BF16),
            dma((3,)),
            *pairs(n_rows),
            *pairs(steps, n_rows),
            *pairs(moves, n_rows),
            *pairs(steps, n_rows // Y_SIZE),
            *pairs(steps, n_rows // Y_SIZE, Y_SIZE),
            *pairs(moves, 2, CHUNKS),
            *pairs(moves, 2),
            *pairs(moves, 2, Y_SIZE),
            *pairs(moves, 2),
        ],
        compiler_params=pltpu.CompilerParams(
            collective_id=0, has_side_effects=True, vmem_limit_bytes=52 << 20
        ),
        cost_estimate=pl.CostEstimate(
            flops=steps * 4 * height * width * width, bytes_accessed=4 * height * width, transcendentals=0
        ),
        name="jacobi",
    )(working, levels)


def solution(mesh):
    placed = (P("rows", "factor"), P(None, "factor", None))
    return jax.shard_map(
        body, mesh=mesh, in_specs=placed, out_specs=P("rows", "factor"), check_vma=False
    )
```
